512 devices in a mesh: dp: 64 (over z, x), tensor: 8 (over y, core).
Axes of the slice: x: 4, y: 4, z: 16, core: 2. Of those that a mesh axis runs over, the one named last changes fastest.
Arguments:
- cache_keys: bfloat16 [256, 1024, 1024], P('dp', 'tensor')
- cache_values: bfloat16 [256, 1024, 1024], P('dp', 'tensor'), may hold values from -6 to 6
- cache_lengths: int32 [256], P('dp'), may hold values from 1 to 1024, as said below
- destination: int32 [256], P('dp'), may hold values from -1 to 127, as said below
- queries: bfloat16 [128, 8192], P('dp')
- new_keys: bfloat16 [128, 1024], P('dp')
- new_values: bfloat16 [128, 1024], P('dp'), may hold values from -6 to 6
Outputs:
- moved_keys: bfloat16 [128, 1024, 1024], P('dp', 'tensor')
- moved_values: bfloat16 [128, 1024, 1024], P('dp', 'tensor')
- attended: bfloat16 [128, 8192], P('dp')
The draws below stay inside these ranges and needn't reach their ends.
Inputs may be any that keep to these rules, and one draw needn't show every extreme that they name: `cache_lengths`: one slot holds exactly 1024 live positions in every draw. `destination`: every survivor index 0 .. 127 is named by exactly one slot and -1 marks a pruned slot. Survivor j is hosted by replica j // 2, so every replica receives exactly 2 survivors; a slot and the survivor it becomes lie on replicas of the same aligned group of 4 replicas along dp, and within a group the survivors follow the order of their slots. A replica keeps from 0 to 4 of its slots.
All inputs are finite; a program needn't handle non-finite values.
Results may differ from the reference program's by a relative error of at most 0.0049.
Values may be sent and summed in bfloat16 or wider, within the bound.
No kernel may reach another device: no remote copies, remote signals or barrier semaphores. Data moves between devices by JAX's collectives and lax.ppermute only.
A program may use at most 64 MiB of HBM per device.

```python
import jax
import jax.numpy as jnp
from jax import lax

QH = 64
KVH = 8
HD = 128
LMAX = 1024
SLOTS = 4
ROWS_DEV = 2
GROUP = 4
SLOTS_ALL = 256
SURV = 128
N_DP = 64
N_TENSOR = 8


def draw_cache_keys(key, part):
    key = jax.random.fold_in(key, 5)
    shape = (SLOTS * N_DP, LMAX, KVH * HD)
    return jax.random.normal(key, shape, jnp.float32).astype(jnp.bfloat16)


def draw_cache_lengths(key, part):
    key = jax.random.fold_in(key, 1)
    count = SLOTS * N_DP
    length_key, pick_key = jax.random.split(key)
    lengths = jax.random.randint(length_key, (count,), 1, LMAX + 1)
    chosen = jax.random.randint(pick_key, (), 0, count)
    return jnp.where(jnp.arange(count) == chosen, LMAX, lengths).astype(jnp.int32)


def draw_destination(key, part):
    key = jax.random.fold_in(key, 2)
    patterns = jnp.array([[4, 3, 1, 0], [4, 2, 2, 0], [4, 4, 0, 0], [3, 3, 2, 0], [4, 2, 1, 1]], jnp.int32)
    blocks = N_DP // GROUP
    pick_key, order_key, slot_key = jax.random.split(key, 3)
    chosen = patterns[jax.random.randint(pick_key, (blocks,), 0, 5)]
    shuffled = jax.vmap(lambda one_key, counts: jax.random.permutation(one_key, counts))(jax.random.split(order_key, blocks), chosen)
    keep_count = shuffled.reshape(N_DP)
    ranks = jax.vmap(lambda one_key: jax.random.permutation(one_key, SLOTS))(jax.random.split(slot_key, N_DP))
    kept = (ranks < keep_count[:, None]).reshape(blocks, GROUP * SLOTS).astype(jnp.int32)
    within = jnp.cumsum(kept, axis=1) - 1
    base = (jnp.arange(blocks, dtype=jnp.int32) * (GROUP * ROWS_DEV))[:, None]
    result = jnp.where(kept > 0, base + within, -1)
    return result.reshape(N_DP * SLOTS).astype(jnp.int32)


def draw_queries(key, part):
    key = jax.random.fold_in(key, 3)
    return jax.random.normal(key, (SURV, QH * HD), jnp.float32).astype(jnp.bfloat16)


def draw_new_keys(key, part):
    key = jax.random.fold_in(key, 4)
    return jax.random.normal(key, (SURV, KVH * HD), jnp.float32).astype(jnp.bfloat16)


def steps_of(own_key, dims, cuts, smallest, largest):
    gain = 1.0
    for dim, blocks in cuts:
        heights = jax.random.uniform(jax.random.fold_in(jax.random.fold_in(own_key, 6), dim), (blocks,), jnp.float32, smallest / len(cuts), largest / len(cuts))
        gain = gain * jnp.repeat(jnp.exp(heights), dims[dim] // blocks).reshape((-1,) + (1,) * (len(dims) - 1 - dim))
    return gain


def bell_draw(rng, extent, scale, limit, pieces=(), held_as=jnp.bfloat16):
    values = jax.random.normal(rng, extent, jnp.float32) * scale
    if len(pieces) > 0:
        values = steps_of(rng, extent, pieces, -0.22, 0.18) * values
    return jnp.clip(values, min=-limit, max=limit).astype(held_as)


def setup_inputs(seed: int = 0) -> dict:
    key_list = jax.random.split(jax.random.key(seed), 8)
    cache_keys = draw_cache_keys(jax.random.fold_in(key_list[7], 71), 0)
    cache_values = bell_draw(key_list[1], (SLOTS_ALL, LMAX, KVH * HD), 1.0, 6.0, ((0, 64), (1, 8)))
    cache_lengths = draw_cache_lengths(jax.random.fold_in(key_list[7], 71), 0)
    destination = draw_destination(jax.random.fold_in(key_list[7], 71), 0)
    queries = draw_queries(jax.random.fold_in(key_list[7], 71), 0)
    new_keys = draw_new_keys(jax.random.fold_in(key_list[7], 71), 0)
    new_values = bell_draw(key_list[6], (SURV, KVH * HD), 1.0, 6.0, ((0, 64),))
    return dict(cache_keys=cache_keys, cache_values=cache_values, cache_lengths=cache_lengths, destination=destination, queries=queries, new_keys=new_keys, new_values=new_values)


floor_score = -1.0e30


def reference(cache_keys, cache_values, cache_lengths, destination, queries, new_keys, new_values):
    slot_count = SLOTS * N_DP
    target = jnp.where(destination >= 0, destination, SURV).astype(jnp.int32)
    source = jnp.zeros((SURV,), jnp.int32).at[target].set(jnp.arange(slot_count, dtype=jnp.int32), mode="drop")
    moved_keys = cache_keys[source]
    moved_values = cache_values[source]
    moved_lengths = cache_lengths[source]
    span_len = LMAX // N_TENSOR
    per_group = QH // KVH
    scale = HD ** -0.5
    position = jnp.arange(LMAX, dtype=jnp.int32).reshape(N_TENSOR, span_len)

    def one_row(items):
        keys, values, length, query, key_new, value_new = items
        grouped = query.astype(jnp.float32).reshape(KVH, per_group, HD)
        block_keys = keys.astype(jnp.float32).reshape(N_TENSOR, span_len, KVH, HD)
        block_values = values.astype(jnp.float32).reshape(N_TENSOR, span_len, KVH, HD)
        scores = jnp.einsum("gqd,blgd->bgql", grouped, block_keys) * scale
        valid = (position < length)[:, None, None, :]
        peak = jnp.max(jnp.where(valid, scores, floor_score), axis=3)
        weights = jnp.where(valid, jnp.exp(scores - peak[..., None]), 0.0).astype(jnp.bfloat16)
        mass = jnp.sum(weights.astype(jnp.float32), axis=3)
        partial_value = jnp.einsum("bgql,blgd->bgqd", weights.astype(jnp.float32), block_values)
        own = jnp.einsum("gqd,gd->gq", grouped, key_new.astype(jnp.float32).reshape(KVH, HD)) * scale
        top = jnp.maximum(jnp.max(peak, axis=0), own)
        own_weight = jnp.exp(own - top)
        fades = jnp.exp(peak - top[None])
        denominator = own_weight + jnp.sum(fades * mass, axis=0)
        own_value = value_new.astype(jnp.float32).reshape(KVH, 1, HD)
        numerator = own_weight[..., None] * own_value + jnp.sum(fades[..., None] * partial_value, axis=0)
        return (numerator / denominator[..., None]).reshape(QH * HD).astype(jnp.bfloat16)

    attended = lax.map(one_row, (moved_keys, moved_values, moved_lengths, queries, new_keys, new_values))
    return moved_keys, moved_values, attended
```

```python
import functools

import jax
import jax.numpy as jnp
from jax import lax
from jax.experimental import pallas as pl
from jax.experimental.pallas import tpu as pltpu
from jax.sharding import Mesh
from jax.sharding import PartitionSpec as P

QH = 64
KVH = 8
HD = 128
SLOTS = 4
ROWS = 2
GROUP = 4
PER = QH // KVH
TENSOR = 8
SPAN = 128
WIDE = KVH * HD
SCALE = HD ** -0.5
FLOOR = -1e30

STAT = ROWS * QH
CHUNK = STAT + QH
ASK = ROWS * QH + 16

EDGE_A = ((0, 1), (1, 0), (2, 3), (3, 2))
EDGE_B = ((1, 2), (2, 1))
EDGE_C = ((1, 3), (2, 0))
RELAY = ((0, 3), (3, 0))

SMEM = pl.BlockSpec(memory_space=pltpu.SMEM)
VMEM = pl.BlockSpec(memory_space=pltpu.VMEM)
ANY = pl.BlockSpec(memory_space=pl.ANY)


def places(dest_ref, slot, first):
    local = dest_ref[slot] - first
    live = dest_ref[slot] >= 0
    return jnp.where(live, lax.shift_right_arithmetic(local, 1), -1), lax.bitwise_and(local, 1)


def copy_all(pairs):
    for guard, copies in pairs:
        @pl.when(guard)
        def _():
            for copy in copies:
                copy.start()
    for guard, copies in pairs:
        @pl.when(guard)
        def _():
            for copy in copies:
                copy.wait()


def send_kernel(wanted, meta_ref, dest_ref, keys_ref, values_ref, *rest):
    outs, sem = rest[:-1], rest[-1]
    z, x = meta_ref[0], meta_ref[1]
    first = z * (GROUP * ROWS)
    pairs = []
    for slot in range(SLOTS):
        host, row = places(dest_ref, slot, first)
        live = host >= 0
        edge = lax.bitwise_xor(host, x)
        for index, (out, (rows, edges)) in enumerate(zip(outs, wanted)):
            guard = edge == edges[0]
            for other in edges[1:]:
                guard = guard | (edge == other)
            guard = guard & live
            if len(rows) == 1:
                guard = guard & (row == rows[0])
                base = 0
            else:
                base = row * 2
            pairs.append((guard, [
                pltpu.make_async_copy(keys_ref.at[slot], out.at[base], sem.at[index, slot, 0]),
                pltpu.make_async_copy(values_ref.at[slot], out.at[base + 1], sem.at[index, slot, 1]),
            ]))
    copy_all(pairs)


def send_buffers(meta, destination, keys, values, wanted):
    return pl.pallas_call(
        functools.partial(send_kernel, wanted),
        out_shape=[jax.ShapeDtypeStruct((2 * len(rows), SPAN, WIDE), jnp.bfloat16) for rows, _ in wanted],
        in_specs=[SMEM, SMEM, ANY, ANY],
        out_specs=[ANY] * len(wanted),
        scratch_shapes=[pltpu.SemaphoreType.DMA((len(wanted), SLOTS, 2))],
        cost_estimate=pl.CostEstimate(flops=0, bytes_accessed=2 * 2**20, transcendentals=0),
    )(meta, destination, keys, values)


def split_three(x):
    high = x.astype(jnp.bfloat16)
    rest = x - high.astype(jnp.float32)
    middle = rest.astype(jnp.bfloat16)
    low = (rest - middle.astype(jnp.float32)).astype(jnp.bfloat16)
    return high.astype(jnp.float32), middle.astype(jnp.float32), low.astype(jnp.float32)


def attend_kernel(meta_ref, dest_ref, length_ref, asked_ref, keys_ref, values_ref, out_ref, keys, values, sem):
    z, x, t = meta_ref[0], meta_ref[1], meta_ref[2]
    first = z * (GROUP * ROWS)
    copies = []
    for slot in range(SLOTS):
        copies.append(pltpu.make_async_copy(keys_ref.at[slot], keys.at[slot], sem.at[0, slot]))
        copies.append(pltpu.make_async_copy(values_ref.at[slot], values.at[slot], sem.at[1, slot]))
    for copy in copies:
        copy.start()
    out_ref[...] = jnp.zeros(out_ref.shape, out_ref.dtype)
    head = lax.broadcasted_iota(jnp.int32, (QH, WIDE), 0)
    lane = lax.broadcasted_iota(jnp.int32, (QH, WIDE), 1)
    diagonal = (head // PER) == (lane // HD)
    position = t * SPAN + lax.broadcasted_iota(jnp.int32, (QH, SPAN), 1)
    column = lax.broadcasted_iota(jnp.int32, (QH, HD), 1)
    for copy in copies:
        copy.wait()
    results = []
    for slot in range(SLOTS):
        host, row = places(dest_ref, slot, first)
        at = pl.multiple_of(jnp.maximum(row, 0) * QH, QH)
        safe = jnp.clip(host, 0, GROUP - 1)
        query = asked_ref[safe, pl.ds(at, QH), :]
        spread = jnp.where(diagonal, jnp.concatenate([query] * KVH, axis=1), jnp.zeros((), jnp.bfloat16))
        scores = lax.dot_general(
            spread, keys[slot], (((1,), (1,)), ((), ())), preferred_element_type=jnp.float32
        ) * SCALE
        valid = position < length_ref[slot]
        peak = jnp.max(jnp.where(valid, scores, FLOOR), axis=1, keepdims=True)
        weights = jnp.where(valid, jnp.exp(scores - peak), 0.0).astype(jnp.bfloat16)
        mass = jnp.sum(weights.astype(jnp.float32), axis=1, keepdims=True)
        full = jnp.dot(weights, values[slot], preferred_element_type=jnp.float32)
        partial = jnp.concatenate(
            [full[g * PER:(g + 1) * PER, g * HD:(g + 1) * HD] for g in range(KVH)], axis=0
        ).astype(jnp.bfloat16)
        stats = jnp.zeros((QH, HD), jnp.float32)
        for k, piece in enumerate(split_three(peak) + split_three(mass)):
            stats = jnp.where(column == row * 8 + k, piece, stats)
        results.append((host, safe, row, at, partial, stats.astype(jnp.bfloat16)))
    for host, safe, row, at, partial, stats in results:
        @pl.when(host >= 0)
        def _(safe=safe, row=row, at=at, partial=partial, stats=stats):
            out_ref[safe, pl.ds(at, QH), :] = partial
            held = out_ref[safe, STAT:CHUNK, :]
            mine = (column >= row * 8) & (column < row * 8 + 8)
            out_ref[safe, STAT:CHUNK, :] = jnp.where(mine, stats, held)


def attend(meta, destination, lengths, asked, keys, values):
    return pl.pallas_call(
        attend_kernel,
        out_shape=jax.ShapeDtypeStruct((GROUP, CHUNK, HD), jnp.bfloat16),
        in_specs=[SMEM, SMEM, SMEM, VMEM, ANY, ANY],
        out_specs=VMEM,
        scratch_shapes=[
            pltpu.VMEM((SLOTS, SPAN, WIDE), jnp.bfloat16),
            pltpu.VMEM((SLOTS, SPAN, WIDE), jnp.bfloat16),
            pltpu.SemaphoreType.DMA((2, SLOTS)),
        ],
        compiler_params=pltpu.CompilerParams(vmem_limit_bytes=16 * 2**20),
        cost_estimate=pl.CostEstimate(flops=2**27, bytes_accessed=2 * 2**20, transcendentals=2**15),
    )(meta, destination, lengths, asked, keys, values)


def origin(group_ref, wanted):
    replica, slot = jnp.int32(0), jnp.int32(0)
    for s in range(GROUP):
        for k in range(SLOTS):
            hit = group_ref[s * SLOTS + k] == wanted
            replica = jnp.where(hit, s, replica)
            slot = jnp.where(hit, k, slot)
    return replica, slot


def pick_kernel(meta_ref, group_ref, got_ref, out_ref):
    z, x = meta_ref[0], meta_ref[1]
    base = z * (GROUP * ROWS) + x * ROWS
    column = lax.broadcasted_iota(jnp.int32, (QH, HD), 1)
    sources = [origin(group_ref, base + row)[0] for row in range(ROWS)]
    for row, source in enumerate(sources):
        out_ref[row * QH:(row + 1) * QH, :] = got_ref[source, row * QH:(row + 1) * QH, :]
    out_ref[STAT:CHUNK, :] = jnp.where(
        column < 8, got_ref[sources[0], STAT:CHUNK, :], got_ref[sources[1], STAT:CHUNK, :]
    )


def pick(meta, group, got):
    return pl.pallas_call(
        pick_kernel,
        out_shape=jax.ShapeDtypeStruct((CHUNK, HD), jnp.bfloat16),
        in_specs=[SMEM, SMEM, VMEM],
        out_specs=VMEM,
    )(meta, group, got)


def finish_kernel(blocks_ref, queries_ref, new_keys_ref, new_values_ref, out_ref):
    for row in range(ROWS):
        def per_head(ref):
            block = ref[row].astype(jnp.float32)
            return jnp.concatenate(
                [jnp.broadcast_to(block[g:g + 1, :], (PER, HD)) for g in range(KVH)], axis=0
            )

        query = queries_ref[row].astype(jnp.float32)
        own = jnp.sum(query * per_head(new_keys_ref), axis=1, keepdims=True) * SCALE
        peaks, masses = [], []
        for b in range(TENSOR):
            stats = blocks_ref[b, STAT:CHUNK, :].astype(jnp.float32)
            piece = [stats[:, row * 8 + k:row * 8 + k + 1] for k in range(6)]
            peaks.append((piece[0] + piece[1]) + piece[2])
            masses.append((piece[3] + piece[4]) + piece[5])
        top = functools.reduce(jnp.maximum, peaks, own)
        own_weight = jnp.exp(own - top)
        denominator = own_weight
        numerator = own_weight * per_head(new_values_ref)
        for b in range(TENSOR):
            fade = jnp.exp(peaks[b] - top)
            denominator = denominator + fade * masses[b]
            numerator = numerator + fade * blocks_ref[b, row * QH:(row + 1) * QH, :].astype(jnp.float32)
        out_ref[row] = (numerator / denominator).astype(jnp.bfloat16)


def finish(blocks, queries, new_keys, new_values):
    return pl.pallas_call(
        finish_kernel,
        out_shape=jax.ShapeDtypeStruct((ROWS, QH, HD), jnp.bfloat16),
        in_specs=[VMEM] * 4,
        out_specs=VMEM,
    )(blocks, queries, new_keys, new_values)


def place_kernel(meta_ref, group_ref, keys_ref, values_ref, a0_ref, a1_ref, b_ref, c0_ref, c1_ref,
                 moved_keys_ref, moved_values_ref, sem):
    z, x = meta_ref[0], meta_ref[1]
    base = z * (GROUP * ROWS) + x * ROWS
    pairs = []
    for row in range(ROWS):
        replica, slot = origin(group_ref, base + row)
        edge = lax.bitwise_xor(replica, x)
        out_keys, out_values = moved_keys_ref.at[row], moved_values_ref.at[row]
        near = (a0_ref, a1_ref)[row]
        far = (c0_ref, c1_ref)[row]
        for which, key_block, value_block in (
            (0, keys_ref.at[slot], values_ref.at[slot]),
            (1, near.at[0], near.at[1]),
            (3, b_ref.at[2 * row], b_ref.at[2 * row + 1]),
            (2, far.at[0], far.at[1]),
        ):
            pairs.append((edge == which, [
                pltpu.make_async_copy(key_block, out_keys, sem.at[row, which, 0]),
                pltpu.make_async_copy(value_block, out_values, sem.at[row, which, 1]),
            ]))
    copy_all(pairs)


def place(meta, group, keys, values, a0, a1, b, c0, c1):
    moved = jax.ShapeDtypeStruct((ROWS, SPAN, WIDE), jnp.bfloat16)
    return pl.pallas_call(
        place_kernel,
        out_shape=[moved, moved],
        in_specs=[SMEM, SMEM] + [ANY] * 7,
        out_specs=[ANY, ANY],
        scratch_shapes=[pltpu.SemaphoreType.DMA((ROWS, 4, 2))],
        cost_estimate=pl.CostEstimate(flops=0, bytes_accessed=2 * 2**20, transcendentals=0),
    )(meta, group, keys, values, a0, a1, b, c0, c1)


def on_device(keys, values, lengths, destination, queries, new_keys, new_values):
    z, x, t = (lax.axis_index(name) for name in ("z", "x", "t"))
    meta = jnp.stack([z, x, t]).astype(jnp.int32)
    first = z * (GROUP * ROWS)
    a1, b = send_buffers(meta, destination, keys, values, (((1,), (1, 2)), ((0, 1), (3,))))
    a0, c0 = send_buffers(meta, destination, keys, values, (((0,), (1,)), ((0,), (2,))))
    a1 = lax.ppermute(a1, "x", EDGE_A)
    b = lax.ppermute(b, "x", EDGE_B)
    c0 = lax.ppermute(c0, "x", EDGE_C)
    a0 = lax.ppermute(a0, "x", EDGE_A)
    c1 = lax.ppermute(a1, "x", RELAY)

    own_queries = queries.reshape(ROWS * QH, HD)
    told = jnp.where(destination >= 0, destination - first, -1).astype(jnp.bfloat16)
    told = jnp.pad(told[None, :], ((0, 15), (0, HD - SLOTS)))
    asked = lax.all_gather(jnp.concatenate([own_queries, told], axis=0), "x")
    group = asked[:, ROWS * QH, :SLOTS].astype(jnp.int32).reshape(GROUP * SLOTS)
    group = jnp.where(group >= 0, group + first, -1)
    sent = attend(meta, destination, lengths, asked, keys, values)
    got = lax.all_to_all(sent, "x", 0, 0)
    mine = pick(meta, group, got)
    blocks = lax.all_gather(mine, "t")
    attended = finish(
        blocks,
        own_queries.reshape(ROWS, QH, HD),
        new_keys.reshape(ROWS, KVH, HD),
        new_values.reshape(ROWS, KVH, HD),
    )
    moved_keys, moved_values = place(meta, group, keys, values, a0, a1, b, c0, c1)
    return moved_keys, moved_values, attended.reshape(ROWS, QH * HD)


def solution(mesh):
    groups = Mesh(mesh.devices.reshape(-1, GROUP, TENSOR), ("z", "x", "t"))
    dp = ("z", "x")
    return jax.shard_map(
        on_device,
        mesh=groups,
        in_specs=(P(dp, "t", None), P(dp, "t", None), P(dp), P(dp), P(dp, None), P(dp, None), P(dp, None)),
        out_specs=(P(dp, "t", None), P(dp, "t", None), P(dp, None)),
        check_vma=False,
    )
```

```python
import functools

import jax
import jax.numpy as jnp
from jax import lax
from jax.experimental import pallas as pl
from jax.experimental.pallas import tpu as pltpu
from jax.sharding import Mesh
from jax.sharding import PartitionSpec as P

QH = 64
KVH = 8
HD = 128
SLOTS = 4
ROWS = 2
GROUP = 4
PER = QH // KVH
TENSOR = 8
SPAN = 128
WIDE = KVH * HD
SCALE = HD ** -0.5
FLOOR = -1e30

STAT = ROWS * QH
PARTIAL = STAT + QH
NOTE = 16

EDGE_A = ((0, 1), (1, 0), (2, 3), (3, 2))
EDGE_B = ((1, 2), (2, 1))
EDGE_C = ((1, 3), (2, 0))
RELAY = ((0, 3), (3, 0))
ASK_C = ((3, 1), (0, 2))

FULL = 60 * 2**20
PART = 16 * 2**20

SMEM = pl.BlockSpec(memory_space=pltpu.SMEM)
VMEM = pl.BlockSpec(memory_space=pltpu.VMEM)
HBM = pl.BlockSpec(memory_space=pltpu.HBM)


def replica_index():
    return lax.axis_index("x")


def first_survivor():
    return lax.axis_index("z") * (GROUP * ROWS)


def places(dest_ref, slot, first):
    local = dest_ref[slot] - first
    live = dest_ref[slot] >= 0
    return jnp.where(live, lax.shift_right_arithmetic(local, 1), -1), lax.bitwise_and(local, 1)


def send_kernel(dest_ref, length_ref, keys_ref, values_ref, a1_ref, a2_ref, b_ref,
                keys, values, note, load_sem, sem, note_sem):
    first, x = first_survivor(), replica_index()
    loads = []
    for slot in range(SLOTS):
        loads.append((
            pltpu.make_async_copy(keys_ref.at[slot], keys.at[slot], load_sem.at[0, slot]),
            pltpu.make_async_copy(values_ref.at[slot], values.at[slot], load_sem.at[1, slot]),
        ))
    for pair in loads:
        for load in pair:
            load.start()
    line = lax.broadcasted_iota(jnp.int32, (NOTE, WIDE), 0)
    guarded = []
    told = [jnp.zeros((NOTE, WIDE), jnp.int32) for _ in range(2)]
    for slot in range(SLOTS):
        host, row = places(dest_ref, slot, first)
        edge = jnp.where(host >= 0, lax.bitwise_xor(host, x), -1)
        along_a = (edge == 1) | (edge == 2)
        along_b = edge == 3
        length = length_ref[slot]
        for n, along in enumerate((along_a, along_b)):
            base = jnp.where(along, row * 3, NOTE)
            for k, value in enumerate((dest_ref[slot] - first + 1, lax.shift_right_logical(length, 4), lax.bitwise_and(length, 15))):
                told[n] = jnp.where(line == base + k, value, told[n])
        for which in range(ROWS):
            mine = row == which
            for guard, out, base in (
                (mine & along_a, (a1_ref, a2_ref)[which], 0),
                (mine & along_b, b_ref, 2 * SPAN * which),
            ):
                guarded.append((guard, slot, [
                    pltpu.make_async_copy(keys.at[slot], out.at[pl.ds(base, SPAN)], sem.at[slot, 0]),
                    pltpu.make_async_copy(values.at[slot], out.at[pl.ds(base + SPAN, SPAN)], sem.at[slot, 1]),
                ]))
    for n in range(2):
        note[n] = told[n].astype(jnp.float32).astype(jnp.bfloat16)
    notes = [
        pltpu.make_async_copy(note.at[0], a2_ref.at[pl.ds(2 * SPAN, NOTE)], note_sem.at[0]),
        pltpu.make_async_copy(note.at[1], b_ref.at[pl.ds(4 * SPAN, NOTE)], note_sem.at[1]),
    ]
    for copy in notes:
        copy.start()
    for slot in range(SLOTS):
        for load in loads[slot]:
            load.wait()
        start_guarded([(guard, copies) for guard, owner, copies in guarded if owner == slot])
    wait_guarded([(guard, copies) for guard, _, copies in guarded])
    for copy in notes:
        copy.wait()


def send_buffers(destination, lengths, keys, values):
    buffer = lambda rows: jax.ShapeDtypeStruct((rows, WIDE), jnp.bfloat16)
    return pl.pallas_call(
        send_kernel,
        out_shape=[buffer(2 * SPAN + NOTE), buffer(2 * SPAN + NOTE), buffer(4 * SPAN + NOTE)],
        in_specs=[SMEM, SMEM, HBM, HBM],
        out_specs=[HBM] * 3,
        scratch_shapes=[
            pltpu.VMEM((SLOTS, SPAN, WIDE), jnp.bfloat16),
            pltpu.VMEM((SLOTS, SPAN, WIDE), jnp.bfloat16),
            pltpu.VMEM((2, NOTE, WIDE), jnp.bfloat16),
            pltpu.SemaphoreType.DMA((2, SLOTS)),
            pltpu.SemaphoreType.DMA((SLOTS, 2)),
            pltpu.SemaphoreType.DMA((2,)),
        ],
        compiler_params=pltpu.CompilerParams(vmem_limit_bytes=FULL),
        cost_estimate=pl.CostEstimate(flops=0, bytes_accessed=4 * 2**20, transcendentals=0),
    )(destination, lengths, keys, values)


def gate_kernel(*refs):
    pass


def gate(held, awaited):
    return pl.pallas_call(
        gate_kernel,
        out_shape=[jax.ShapeDtypeStruct(one.shape, one.dtype) for one in held],
        in_specs=[HBM] * (len(held) + len(awaited)),
        out_specs=[HBM] * len(held),
        input_output_aliases={n: n for n in range(len(held))},
        compiler_params=pltpu.CompilerParams(vmem_limit_bytes=FULL),
        cost_estimate=pl.CostEstimate(flops=0, bytes_accessed=0, transcendentals=0),
    )(*held, *awaited)


def start_guarded(guarded):
    for guard, copies in guarded:
        @pl.when(guard)
        def _(copies=copies):
            for copy in copies:
                copy.start()


def wait_guarded(guarded):
    for guard, copies in guarded:
        @pl.when(guard)
        def _(copies=copies):
            for copy in copies:
                copy.wait()


def split_three(x):
    high = x.astype(jnp.bfloat16)
    rest = x - high.astype(jnp.float32)
    middle = rest.astype(jnp.bfloat16)
    low = (rest - middle.astype(jnp.float32)).astype(jnp.bfloat16)
    return high.astype(jnp.float32), middle.astype(jnp.float32), low.astype(jnp.float32)


def heads_of(ref, row):
    block = ref[...].astype(jnp.float32)
    return jnp.concatenate([block[row:row + 1, h * HD:(h + 1) * HD] for h in range(QH)], axis=0)


def spread_heads(query):
    head = lax.broadcasted_iota(jnp.int32, (QH, WIDE), 0)
    lane = lax.broadcasted_iota(jnp.int32, (QH, WIDE), 1)
    wide = jnp.concatenate([query] * KVH, axis=1)
    return jnp.where((head // PER) == (lane // HD), wide, 0.0).astype(jnp.bfloat16)


def block_attention(query, keys, values, length):
    position = lax.axis_index("t") * SPAN + lax.broadcasted_iota(jnp.int32, (QH, SPAN), 1)
    scores = lax.dot_general(
        spread_heads(query), keys, (((1,), (1,)), ((), ())), preferred_element_type=jnp.float32
    ) * SCALE
    valid = position < length
    peak = jnp.max(jnp.where(valid, scores, FLOOR), axis=1, keepdims=True)
    weights = jnp.where(valid, jnp.exp(scores - peak), 0.0).astype(jnp.bfloat16)
    mass = jnp.sum(weights.astype(jnp.float32), axis=1, keepdims=True)
    full = jnp.dot(weights, values, preferred_element_type=jnp.float32)
    partial = jnp.concatenate([full[g * PER:(g + 1) * PER, g * HD:(g + 1) * HD] for g in range(KVH)], axis=0)
    return peak, mass, partial.astype(jnp.bfloat16)


def statistics(row, peak, mass, held):
    column = lax.broadcasted_iota(jnp.int32, (QH, HD), 1)
    for k, piece in enumerate(split_three(peak) + split_three(mass)):
        held = jnp.where(column == row * 8 + k, piece, held)
    return held


def early_kernel(dest_ref, length_ref, asked_ref, queries_ref, new_keys_ref, new_values_ref, keys_ref, values_ref,
                 far_ref, own_ref, own_values_ref, keys, values, sem):
    first, x = first_survivor(), replica_index()
    line = lax.broadcasted_iota(jnp.int32, (NOTE, HD), 0)
    told = jnp.zeros((NOTE, HD), jnp.int32)
    far = []
    guarded = []
    for row in range(ROWS):
        found, length = jnp.int32(-1), jnp.int32(0)
        wanted = lax.bitwise_xor(x, 2) * ROWS + row + first
        for slot in range(SLOTS):
            hit = dest_ref[slot] == wanted
            found = jnp.where(hit, slot, found)
            length = jnp.where(hit, length_ref[slot], length)
        told = jnp.where((line == row * 3) & (found >= 0), wanted - first + 1, told)
        slot = jnp.maximum(found, 0)
        guarded.append((found >= 0, [
            pltpu.make_async_copy(keys_ref.at[slot], keys.at[row], sem.at[row, 0]),
            pltpu.make_async_copy(values_ref.at[slot], values.at[row], sem.at[row, 1]),
        ]))
        far.append((found, length))
    start_guarded(guarded)
    far_ref[PARTIAL:, :] = told.astype(jnp.float32).astype(jnp.bfloat16)
    far_ref[STAT:PARTIAL, :] = jnp.zeros((QH, HD), jnp.bfloat16)
    for row in range(ROWS):
        def per_head(ref):
            block = ref[...].astype(jnp.float32)
            return jnp.concatenate([
                jnp.broadcast_to(block[row:row + 1, g * HD:(g + 1) * HD], (PER, HD)) for g in range(KVH)
            ], axis=0)

        own = jnp.sum(heads_of(queries_ref, row) * per_head(new_keys_ref), axis=1, keepdims=True) * SCALE
        own_ref[row] = jnp.broadcast_to(own, (QH, HD))
        own_values_ref[row] = per_head(new_values_ref)
    wait_guarded(guarded)
    for row, (found, length) in enumerate(far):
        @pl.when(found >= 0)
        def _(row=row, length=length):
            peak, mass, partial = block_attention(heads_of(asked_ref, row), keys[row], values[row], length)
            far_ref[row * QH:(row + 1) * QH, :] = partial
            held = far_ref[STAT:PARTIAL, :].astype(jnp.float32)
            far_ref[STAT:PARTIAL, :] = statistics(row, peak, mass, held).astype(jnp.bfloat16)


def early(destination, lengths, asked, queries, new_keys, new_values, keys, values):
    own = jax.ShapeDtypeStruct((ROWS, QH, HD), jnp.float32)
    return pl.pallas_call(
        early_kernel,
        out_shape=[jax.ShapeDtypeStruct((PARTIAL + NOTE, HD), jnp.bfloat16), own, own],
        in_specs=[SMEM, SMEM] + [VMEM] * 4 + [HBM] * 2,
        out_specs=[VMEM] * 3,
        scratch_shapes=[
            pltpu.VMEM((ROWS, SPAN, WIDE), jnp.bfloat16),
            pltpu.VMEM((ROWS, SPAN, WIDE), jnp.bfloat16),
            pltpu.SemaphoreType.DMA((ROWS, 2)),
        ],
        compiler_params=pltpu.CompilerParams(vmem_limit_bytes=FULL),
        cost_estimate=pl.CostEstimate(flops=2**26, bytes_accessed=2**20, transcendentals=2**14),
    )(destination, lengths, asked, queries, new_keys, new_values, keys, values)


def attend_kernel(dest_ref, length_ref, queries_ref, keys_ref, values_ref, a1_ref, a2_ref, b_ref, far_ref,
                  out_ref, moved_keys_ref, moved_values_ref, stage, sem, moved_sem):
    first, x = first_survivor(), replica_index()
    note_a = a2_ref[2 * SPAN:, :HD].astype(jnp.float32)
    note_b = b_ref[4 * SPAN:, :HD].astype(jnp.float32)
    line = lax.broadcasted_iota(jnp.int32, (NOTE, HD), 0)
    rows = []
    guarded = []
    for row in range(ROWS):
        wanted = x * ROWS + row
        here, slot, length = jnp.bool_(False), jnp.int32(0), jnp.int32(0)
        for k in range(SLOTS):
            hit = dest_ref[k] == wanted + first
            here = here | hit
            slot = jnp.where(hit, k, slot)
            length = jnp.where(hit, length_ref[k], length)

        def read(note, k):
            return jnp.max(jnp.where(line == row * 3 + k, note, 0.0)).astype(jnp.int32)

        in_a, in_b = read(note_a, 0) == wanted + 1, read(note_b, 0) == wanted + 1
        length = jnp.where(in_a, read(note_a, 1) * 16 + read(note_a, 2), length)
        length = jnp.where(in_b, read(note_b, 1) * 16 + read(note_b, 2), length)
        rows.append((here | in_a | in_b, length))
        base = 2 * SPAN * row
        whole = stage.at[pl.ds(base, 2 * SPAN)]
        guarded.append((here, [
            pltpu.make_async_copy(keys_ref.at[slot], stage.at[pl.ds(base, SPAN)], sem.at[row, 0]),
            pltpu.make_async_copy(values_ref.at[slot], stage.at[pl.ds(base + SPAN, SPAN)], sem.at[row, 1]),
        ]))
        guarded.append((in_a, [
            pltpu.make_async_copy((a1_ref, a2_ref)[row].at[pl.ds(0, 2 * SPAN)], whole, sem.at[row, 0])
        ]))
        guarded.append((in_b, [pltpu.make_async_copy(b_ref.at[pl.ds(base, 2 * SPAN)], whole, sem.at[row, 0])]))
    start_guarded(guarded)
    out_ref[...] = far_ref[:PARTIAL, :]
    wait_guarded(guarded)
    moves = []
    for row, (near, _) in enumerate(rows):
        base = 2 * SPAN * row
        moves.append((near, [
            pltpu.make_async_copy(stage.at[pl.ds(base, SPAN)], moved_keys_ref.at[row], moved_sem.at[row, 0]),
            pltpu.make_async_copy(stage.at[pl.ds(base + SPAN, SPAN)], moved_values_ref.at[row], moved_sem.at[row, 1]),
        ]))
    start_guarded(moves)
    results = [
        block_attention(
            heads_of(queries_ref, row), stage[2 * SPAN * row:2 * SPAN * row + SPAN],
            stage[2 * SPAN * row + SPAN:2 * SPAN * (row + 1)], length,
        )
        for row, (_, length) in enumerate(rows)
    ]
    for row, ((near, _), (peak, mass, partial)) in enumerate(zip(rows, results)):
        @pl.when(near)
        def _(row=row, peak=peak, mass=mass, partial=partial):
            out_ref[row * QH:(row + 1) * QH, :] = partial
            held = out_ref[STAT:PARTIAL, :].astype(jnp.float32)
            out_ref[STAT:PARTIAL, :] = statistics(row, peak, mass, held).astype(jnp.bfloat16)
    wait_guarded(moves)


def attend(destination, lengths, queries, keys, values, a1, a2, b, far):
    moved = jax.ShapeDtypeStruct((ROWS, SPAN, WIDE), jnp.bfloat16)
    return pl.pallas_call(
        attend_kernel,
        out_shape=[jax.ShapeDtypeStruct((PARTIAL, HD), jnp.bfloat16), moved, moved],
        in_specs=[SMEM, SMEM, VMEM, HBM, HBM, HBM, VMEM, VMEM, VMEM],
        out_specs=[VMEM, HBM, HBM],
        scratch_shapes=[
            pltpu.VMEM((4 * SPAN, WIDE), jnp.bfloat16),
            pltpu.SemaphoreType.DMA((ROWS, 2)),
            pltpu.SemaphoreType.DMA((ROWS, 2)),
        ],
        compiler_params=pltpu.CompilerParams(vmem_limit_bytes=PART),
        cost_estimate=pl.CostEstimate(flops=2**34, bytes_accessed=2 * 2**20, transcendentals=2**14),
    )(destination, lengths, queries, keys, values, a1, a2, b, far)


def finish_kernel(far_ref, blocks_ref, own_ref, own_values_ref, c1_ref, c2_ref, keys_in_ref, values_in_ref,
                  attended_ref, moved_keys_ref, moved_values_ref, sem):
    x = replica_index()
    note = far_ref[PARTIAL:, :].astype(jnp.float32)
    line = lax.broadcasted_iota(jnp.int32, (NOTE, HD), 0)
    guarded = []
    for row, buffer in enumerate((c1_ref, c2_ref)):
        told = jnp.max(jnp.where(line == row * 3, note, 0.0)).astype(jnp.int32)
        guarded.append((told == x * ROWS + row + 1, [
            pltpu.make_async_copy(buffer.at[pl.ds(0, SPAN)], moved_keys_ref.at[row], sem.at[row, 0]),
            pltpu.make_async_copy(buffer.at[pl.ds(SPAN, SPAN)], moved_values_ref.at[row], sem.at[row, 1]),
        ]))
    start_guarded(guarded)
    column = lax.broadcasted_iota(jnp.int32, (QH, HD), 1)
    own = jnp.where(column < 8, own_ref[0], own_ref[1])
    joined = []
    for b in range(TENSOR):
        stats = blocks_ref[b, STAT:PARTIAL, :].astype(jnp.float32)
        joined.append((stats + pltpu.roll(stats, HD - 1, 1)) + pltpu.roll(stats, HD - 2, 1))
    top = functools.reduce(jnp.maximum, joined, own)
    own_weight = jnp.exp(own - top)
    fades = [jnp.exp(part - top) for part in joined]
    denominator = own_weight
    for part, fade in zip(joined, fades):
        denominator = denominator + fade * pltpu.roll(part, HD - 3, 1)
    parts = []
    for row in range(ROWS):
        pick = slice(row * 8, row * 8 + 1)
        total = own_weight[:, pick] * own_values_ref[row]
        for b in range(TENSOR):
            total = total + fades[b][:, pick] * blocks_ref[b, row * QH:(row + 1) * QH, :].astype(jnp.float32)
        parts.append(total / denominator[:, pick])
    for head in range(QH):
        both = jnp.concatenate([part[head:head + 1] for part in parts], axis=0)
        attended_ref[:, head * HD:(head + 1) * HD] = both.astype(jnp.bfloat16)
    wait_guarded(guarded)


def finish(far, blocks, own, own_values, c1, c2, moved_keys, moved_values):
    moved = jax.ShapeDtypeStruct((ROWS, SPAN, WIDE), jnp.bfloat16)
    return pl.pallas_call(
        finish_kernel,
        out_shape=[jax.ShapeDtypeStruct((ROWS, QH * HD), jnp.bfloat16), moved, moved],
        in_specs=[VMEM] * 6 + [HBM] * 2,
        out_specs=[VMEM, HBM, HBM],
        input_output_aliases={6: 1, 7: 2},
        scratch_shapes=[pltpu.SemaphoreType.DMA((ROWS, 2))],
        compiler_params=pltpu.CompilerParams(vmem_limit_bytes=PART),
        cost_estimate=pl.CostEstimate(flops=2**20, bytes_accessed=2**20, transcendentals=2**16),
    )(far, blocks, own, own_values, c1, c2, moved_keys, moved_values)


def on_device(keys, values, lengths, destination, queries, new_keys, new_values):
    asked = lax.ppermute(queries, "x", ASK_C)
    a1, a2, b = gate(send_buffers(destination, lengths, keys, values), (asked,))
    a1 = lax.ppermute(a1, "x", EDGE_A)
    a2 = lax.ppermute(a2, "x", EDGE_A)
    b = lax.ppermute(b, "x", EDGE_B)
    far, own, own_values = early(destination, lengths, asked, queries, new_keys, new_values, keys, values)
    far = lax.ppermute(far, "x", EDGE_C)
    c1 = lax.ppermute(a1, "x", RELAY)
    c2 = lax.ppermute(a2, "x", RELAY)
    partial, moved_keys, moved_values = attend(destination, lengths, queries, keys, values, a1, a2, b, far)
    blocks = lax.all_gather(partial, "t")
    attended, moved_keys, moved_values = finish(far, blocks, own, own_values, c1, c2, moved_keys, moved_values)
    return moved_keys, moved_values, attended


def solution(mesh):
    groups = Mesh(mesh.devices.reshape(-1, GROUP, TENSOR), ("z", "x", "t"))
    dp = ("z", "x")
    return jax.shard_map(
        on_device,
        mesh=groups,
        in_specs=(P(dp, "t", None), P(dp, "t", None), P(dp), P(dp), P(dp, None), P(dp, None), P(dp, None)),
        out_specs=(P(dp, "t", None), P(dp, "t", None), P(dp, None)),
        check_vma=False,
    )
```

```python
import functools

import jax
import jax.numpy as jnp
from jax import lax
from jax.experimental import pallas as pl
from jax.experimental.pallas import tpu as pltpu
from jax.sharding import Mesh
from jax.sharding import PartitionSpec as P

QH = 64
KVH = 8
HD = 128
SLOTS = 4
ROWS = 2
GROUP = 4
PER = QH // KVH
TENSOR = 8
SPAN = 128
WIDE = KVH * HD
SCALE = HD ** -0.5
FLOOR = -1e30

STAT = ROWS * QH
STATS = 6
PARTIAL = STAT + 16
NOTE = 16
EDGE_A = ((0, 1), (1, 0), (2, 3), (3, 2))
EDGE_B = ((1, 2), (2, 1))
EDGE_C = ((1, 3), (2, 0))
RELAY = ((0, 3), (3, 0))
ASK_C = ((3, 1), (0, 2))

FULL = 60 * 2**20
PART = 16 * 2**20

SMEM = pl.BlockSpec(memory_space=pltpu.SMEM)
VMEM = pl.BlockSpec(memory_space=pltpu.VMEM)
HBM = pl.BlockSpec(memory_space=pltpu.HBM)


def replica_index():
    return lax.axis_index("x")


def first_survivor():
    return lax.axis_index("z") * (GROUP * ROWS)


def places(dest_ref, slot, first):
    local = dest_ref[slot] - first
    live = dest_ref[slot] >= 0
    return jnp.where(live, lax.shift_right_arithmetic(local, 1), -1), lax.bitwise_and(local, 1)


def along_a_places(row, a1_ref, a2_ref):
    if row == 0:
        return a1_ref.at[pl.ds(0, SPAN)], a1_ref.at[pl.ds(SPAN, SPAN)]
    return a1_ref.at[pl.ds(2 * SPAN, SPAN)], a2_ref.at[pl.ds(0, SPAN)]


def along_b_places(row, b1_ref, b2_ref):
    buffer = (b1_ref, b2_ref)[row]
    return buffer.at[pl.ds(0, SPAN)], buffer.at[pl.ds(SPAN, SPAN)]


def send_kernel(dest_ref, length_ref, keys_ref, values_ref, queries_ref, a1_ref, a2_ref, b1_ref, b2_ref, ask_ref,
                keys, values, note, load_sem, sem, note_sem):
    first, x = first_survivor(), replica_index()
    loads = []
    for slot in range(SLOTS):
        loads.append((
            pltpu.make_async_copy(keys_ref.at[slot], keys.at[slot], load_sem.at[0, slot]),
            pltpu.make_async_copy(values_ref.at[slot], values.at[slot], load_sem.at[1, slot]),
        ))
    for pair in loads:
        for load in pair:
            load.start()
    line = lax.broadcasted_iota(jnp.int32, (NOTE, WIDE), 0)
    guarded = []
    told = [jnp.zeros((NOTE, WIDE), jnp.int32) for _ in range(2)]
    for slot in range(SLOTS):
        host, row = places(dest_ref, slot, first)
        edge = jnp.where(host >= 0, lax.bitwise_xor(host, x), -1)
        along_a = (edge == 1) | (edge == 2)
        along_b = edge == 3
        length = length_ref[slot]
        for n, along in enumerate((along_a, along_b)):
            base = jnp.where(along, row * 3, NOTE)
            for k, value in enumerate((dest_ref[slot] - first + 1, lax.shift_right_logical(length, 4), lax.bitwise_and(length, 15))):
                told[n] = jnp.where(line == base + k, value, told[n])
        for which in range(ROWS):
            mine = row == which
            for guard, to_keys, to_values in (
                (mine & along_a,) + along_a_places(which, a1_ref, a2_ref),
                (mine & along_b,) + along_b_places(which, b1_ref, b2_ref),
            ):
                guarded.append((guard, slot, [
                    pltpu.make_async_copy(keys.at[slot], to_keys, sem.at[slot, 0]),
                    pltpu.make_async_copy(values.at[slot], to_values, sem.at[slot, 1]),
                ]))
    for n in range(2):
        note[n] = told[n].astype(jnp.float32).astype(jnp.bfloat16)
    notes = [
        pltpu.make_async_copy(note.at[0], a2_ref.at[pl.ds(SPAN, NOTE)], note_sem.at[0]),
        pltpu.make_async_copy(note.at[1], b2_ref.at[pl.ds(2 * SPAN, NOTE)], note_sem.at[1]),
    ]
    notes.append(pltpu.make_async_copy(queries_ref, ask_ref, note_sem.at[2]))
    for copy in notes:
        copy.start()
    for slot in range(SLOTS):
        for load in loads[slot]:
            load.wait()
        start_guarded([(guard, copies) for guard, owner, copies in guarded if owner == slot])
    wait_guarded([(guard, copies) for guard, _, copies in guarded])
    for copy in notes:
        copy.wait()


def send_buffers(destination, lengths, keys, values, queries):
    buffer = lambda rows: jax.ShapeDtypeStruct((rows, WIDE), jnp.bfloat16)
    return pl.pallas_call(
        send_kernel,
        out_shape=[
            buffer(3 * SPAN), buffer(SPAN + NOTE), buffer(2 * SPAN), buffer(2 * SPAN + NOTE),
            jax.ShapeDtypeStruct(queries.shape, queries.dtype),
        ],
        in_specs=[SMEM, SMEM, HBM, HBM, VMEM],
        out_specs=[HBM] * 5,
        scratch_shapes=[
            pltpu.VMEM((SLOTS, SPAN, WIDE), jnp.bfloat16),
            pltpu.VMEM((SLOTS, SPAN, WIDE), jnp.bfloat16),
            pltpu.VMEM((2, NOTE, WIDE), jnp.bfloat16),
            pltpu.SemaphoreType.DMA((2, SLOTS)),
            pltpu.SemaphoreType.DMA((SLOTS, 2)),
            pltpu.SemaphoreType.DMA((3,)),
        ],
        compiler_params=pltpu.CompilerParams(vmem_limit_bytes=FULL),
        cost_estimate=pl.CostEstimate(flops=0, bytes_accessed=4 * 2**20, transcendentals=0),
    )(destination, lengths, keys, values, queries)


def start_guarded(guarded):
    for guard, copies in guarded:
        @pl.when(guard)
        def _(copies=copies):
            for copy in copies:
                copy.start()


def wait_guarded(guarded):
    for guard, copies in guarded:
        @pl.when(guard)
        def _(copies=copies):
            for copy in copies:
                copy.wait()


def split_three(x):
    high = x.astype(jnp.bfloat16)
    rest = x - high.astype(jnp.float32)
    middle = rest.astype(jnp.bfloat16)
    low = (rest - middle.astype(jnp.float32)).astype(jnp.bfloat16)
    return high.astype(jnp.float32), middle.astype(jnp.float32), low.astype(jnp.float32)


def heads_of(ref, row):
    block = ref[...].astype(jnp.float32)
    return jnp.concatenate([block[row:row + 1, h * HD:(h + 1) * HD] for h in range(QH)], axis=0)


def spread_heads(query):
    head = lax.broadcasted_iota(jnp.int32, (QH, WIDE), 0)
    lane = lax.broadcasted_iota(jnp.int32, (QH, WIDE), 1)
    wide = jnp.concatenate([query] * KVH, axis=1)
    return jnp.where((head // PER) == (lane // HD), wide, 0.0).astype(jnp.bfloat16)


def block_attention(query, keys, values, length):
    position = lax.axis_index("t") * SPAN + lax.broadcasted_iota(jnp.int32, (QH, SPAN), 1)
    scores = lax.dot_general(
        spread_heads(query), keys, (((1,), (1,)), ((), ())), preferred_element_type=jnp.float32
    ) * SCALE
    valid = position < length
    peak = jnp.max(jnp.where(valid, scores, FLOOR), axis=1, keepdims=True)
    weights = jnp.where(valid, jnp.exp(scores - peak), 0.0).astype(jnp.bfloat16)
    mass = jnp.sum(weights.astype(jnp.float32), axis=1, keepdims=True)
    full = jnp.dot(weights, values, preferred_element_type=jnp.float32)
    partial = jnp.concatenate([full[g * PER:(g + 1) * PER, g * HD:(g + 1) * HD] for g in range(KVH)], axis=0)
    return peak, mass, partial.astype(jnp.bfloat16)


def flip(columns):
    lane = lax.broadcasted_iota(jnp.int32, (QH, HD), 1)
    block = jnp.zeros((QH, HD), jnp.float32)
    for n, column in columns.items():
        block = jnp.where(lane == n, column, block)
    return jnp.transpose(jnp.concatenate([block, jnp.zeros((HD - QH, HD), jnp.float32)], axis=0))


def statistics(row, peak, mass):
    columns = {row * STATS + k: piece for k, piece in enumerate(split_three(peak) + split_three(mass))}
    return flip(columns)[:16].astype(jnp.bfloat16)


def mine(row):
    line = lax.broadcasted_iota(jnp.int32, (16, HD), 0)
    return (line >= row * STATS) & (line < (row + 1) * STATS)


def early_kernel(dest_ref, length_ref, asked_ref, queries_ref, new_keys_ref, new_values_ref, keys_ref, values_ref,
                 far_ref, own_ref, own_values_ref, keys, values, sem):
    first, x = first_survivor(), replica_index()
    line = lax.broadcasted_iota(jnp.int32, (NOTE, HD), 0)
    told = jnp.zeros((NOTE, HD), jnp.int32)
    far = []
    guarded = []
    for row in range(ROWS):
        found, length = jnp.int32(-1), jnp.int32(0)
        wanted = lax.bitwise_xor(x, 2) * ROWS + row + first
        for slot in range(SLOTS):
            hit = dest_ref[slot] == wanted
            found = jnp.where(hit, slot, found)
            length = jnp.where(hit, length_ref[slot], length)
        told = jnp.where((line == row * 3) & (found >= 0), wanted - first + 1, told)
        slot = jnp.maximum(found, 0)
        guarded.append((found >= 0, [
            pltpu.make_async_copy(keys_ref.at[slot], keys.at[row], sem.at[row, 0]),
            pltpu.make_async_copy(values_ref.at[slot], values.at[row], sem.at[row, 1]),
        ]))
        far.append((found, length))
    start_guarded(guarded)
    far_ref[PARTIAL:, :] = told.astype(jnp.float32).astype(jnp.bfloat16)
    far_ref[STAT:PARTIAL, :] = jnp.zeros((16, HD), jnp.bfloat16)
    own = {}
    for row in range(ROWS):
        def per_head(ref):
            block = ref[...].astype(jnp.float32)
            return jnp.concatenate([
                jnp.broadcast_to(block[row:row + 1, g * HD:(g + 1) * HD], (PER, HD)) for g in range(KVH)
            ], axis=0)

        own[row] = jnp.sum(heads_of(queries_ref, row) * per_head(new_keys_ref), axis=1, keepdims=True) * SCALE
        own_values_ref[row] = per_head(new_values_ref)
    own_ref[...] = flip(own)[:8]
    wait_guarded(guarded)
    for row, (found, length) in enumerate(far):
        @pl.when(found >= 0)
        def _(row=row, length=length):
            peak, mass, partial = block_attention(heads_of(asked_ref, row), keys[row], values[row], length)
            far_ref[row * QH:(row + 1) * QH, :] = partial
            far_ref[STAT:PARTIAL, :] = jnp.where(mine(row), statistics(row, peak, mass), far_ref[STAT:PARTIAL, :])


def early(destination, lengths, asked, queries, new_keys, new_values, keys, values):
    return pl.pallas_call(
        early_kernel,
        out_shape=[
            jax.ShapeDtypeStruct((PARTIAL + NOTE, HD), jnp.bfloat16),
            jax.ShapeDtypeStruct((8, HD), jnp.float32),
            jax.ShapeDtypeStruct((ROWS, QH, HD), jnp.float32),
        ],
        in_specs=[SMEM, SMEM] + [VMEM] * 4 + [HBM] * 2,
        out_specs=[VMEM] * 3,
        scratch_shapes=[
            pltpu.VMEM((ROWS, SPAN, WIDE), jnp.bfloat16),
            pltpu.VMEM((ROWS, SPAN, WIDE), jnp.bfloat16),
            pltpu.SemaphoreType.DMA((ROWS, 2)),
        ],
        compiler_params=pltpu.CompilerParams(vmem_limit_bytes=PART),
        cost_estimate=pl.CostEstimate(flops=2**32, bytes_accessed=2**20, transcendentals=2**14),
    )(destination, lengths, asked, queries, new_keys, new_values, keys, values)


def attend_kernel(dest_ref, length_ref, queries_ref, keys_ref, values_ref, a1_ref, a2_ref, b1_ref, b2_ref, far_ref,
                  out_ref, moved_keys_ref, moved_values_ref, stage, pack, sem, moved_sem):
    first, x = first_survivor(), replica_index()
    note_a = a2_ref[SPAN:, :HD].astype(jnp.float32)
    note_b = b2_ref[2 * SPAN:, :HD].astype(jnp.float32)
    line = lax.broadcasted_iota(jnp.int32, (NOTE, HD), 0)
    rows = []
    guarded = []
    for row in range(ROWS):
        wanted = x * ROWS + row
        here, slot, length = jnp.bool_(False), jnp.int32(0), jnp.int32(0)
        for k in range(SLOTS):
            hit = dest_ref[k] == wanted + first
            here = here | hit
            slot = jnp.where(hit, k, slot)
            length = jnp.where(hit, length_ref[k], length)

        def read(note, k):
            return jnp.max(jnp.where(line == row * 3 + k, note, 0.0)).astype(jnp.int32)

        in_a, in_b = read(note_a, 0) == wanted + 1, read(note_b, 0) == wanted + 1
        length = jnp.where(in_a, read(note_a, 1) * 16 + read(note_a, 2), length)
        length = jnp.where(in_b, read(note_b, 1) * 16 + read(note_b, 2), length)
        rows.append((here | in_a | in_b, length))
        base = 2 * SPAN * row
        for guard, from_keys, from_values in (
            (here, keys_ref.at[slot], values_ref.at[slot]),
            (in_a,) + along_a_places(row, a1_ref, a2_ref),
            (in_b,) + along_b_places(row, b1_ref, b2_ref),
        ):
            guarded.append((guard, [
                pltpu.make_async_copy(from_keys, stage.at[pl.ds(base, SPAN)], sem.at[row, 0]),
                pltpu.make_async_copy(from_values, stage.at[pl.ds(base + SPAN, SPAN)], sem.at[row, 1]),
            ]))
    start_guarded(guarded)
    pack[...] = far_ref[:PARTIAL, :]
    wait_guarded(guarded)
    moves = []
    for row, (near, _) in enumerate(rows):
        base = 2 * SPAN * row
        moves.append((near, [
            pltpu.make_async_copy(stage.at[pl.ds(base, SPAN)], moved_keys_ref.at[row], moved_sem.at[row, 0]),
            pltpu.make_async_copy(stage.at[pl.ds(base + SPAN, SPAN)], moved_values_ref.at[row], moved_sem.at[row, 1]),
        ]))
    start_guarded(moves)
    results = [
        block_attention(
            heads_of(queries_ref, row), stage[2 * SPAN * row:2 * SPAN * row + SPAN],
            stage[2 * SPAN * row + SPAN:2 * SPAN * (row + 1)], length,
        )
        for row, (_, length) in enumerate(rows)
    ]
    for row, ((near, _), (peak, mass, partial)) in enumerate(zip(rows, results)):
        @pl.when(near)
        def _(row=row, peak=peak, mass=mass, partial=partial):
            pack[row * QH:(row + 1) * QH, :] = partial
            pack[STAT:PARTIAL, :] = jnp.where(mine(row), statistics(row, peak, mass), pack[STAT:PARTIAL, :])
    for peer in range(TENSOR):
        out_ref[peer] = pack[...]
    wait_guarded(moves)


def attend(destination, lengths, queries, keys, values, a1, a2, b1, b2, far):
    moved = jax.ShapeDtypeStruct((ROWS, SPAN, WIDE), jnp.bfloat16)
    return pl.pallas_call(
        attend_kernel,
        out_shape=[jax.ShapeDtypeStruct((TENSOR, PARTIAL, HD), jnp.bfloat16), moved, moved],
        in_specs=[SMEM, SMEM, VMEM, HBM, HBM, HBM, VMEM, HBM, VMEM, VMEM],
        out_specs=[VMEM, HBM, HBM],
        scratch_shapes=[
            pltpu.VMEM((4 * SPAN, WIDE), jnp.bfloat16),
            pltpu.VMEM((PARTIAL, HD), jnp.bfloat16),
            pltpu.SemaphoreType.DMA((ROWS, 2)),
            pltpu.SemaphoreType.DMA((ROWS, 2)),
        ],
        compiler_params=pltpu.CompilerParams(vmem_limit_bytes=PART),
        cost_estimate=pl.CostEstimate(flops=2**32, bytes_accessed=2 * 2**20, transcendentals=2**14),
    )(destination, lengths, queries, keys, values, a1, a2, b1, b2, far)


def finish_kernel(far_ref, blocks_ref, own_ref, own_values_ref, c1_ref, c2_ref, keys_in_ref, values_in_ref,
                  attended_ref, moved_keys_ref, moved_values_ref, sem):
    x = replica_index()
    note = far_ref[PARTIAL:, :].astype(jnp.float32)
    line = lax.broadcasted_iota(jnp.int32, (NOTE, HD), 0)
    guarded = []
    for row in range(ROWS):
        told = jnp.max(jnp.where(line == row * 3, note, 0.0)).astype(jnp.int32)
        from_keys, from_values = along_a_places(row, c1_ref, c2_ref)
        guarded.append((told == x * ROWS + row + 1, [
            pltpu.make_async_copy(from_keys, moved_keys_ref.at[row], sem.at[row, 0]),
            pltpu.make_async_copy(from_values, moved_values_ref.at[row], sem.at[row, 1]),
        ]))
    start_guarded(guarded)
    stats = [blocks_ref[b, STAT:PARTIAL, :].astype(jnp.float32) for b in range(TENSOR)]
    columns = []
    for row in range(ROWS):
        at = row * STATS
        peaks = [(one[at:at + 1] + one[at + 1:at + 2]) + one[at + 2:at + 3] for one in stats]
        masses = [(one[at + 3:at + 4] + one[at + 4:at + 5]) + one[at + 5:at + 6] for one in stats]
        own = own_ref[row:row + 1, :]
        top = functools.reduce(jnp.maximum, peaks, own)
        fades = [jnp.exp(peak - top) for peak in peaks]
        own_weight = jnp.exp(own - top)
        denominator = own_weight
        for fade, mass in zip(fades, masses):
            denominator = denominator + fade * mass
        columns += [one / denominator for one in fades + [own_weight]]
    columns.append(jnp.zeros((HD - len(columns), HD), jnp.float32))
    shares = jnp.transpose(jnp.concatenate(columns, axis=0))[:QH]
    parts = []
    for row in range(ROWS):
        at = row * (TENSOR + 1)
        total = shares[:, at + TENSOR:at + TENSOR + 1] * own_values_ref[row]
        for b in range(TENSOR):
            total = total + shares[:, at + b:at + b + 1] * blocks_ref[b, row * QH:(row + 1) * QH, :].astype(jnp.float32)
        parts.append(total)
    for head in range(QH):
        both = jnp.concatenate([part[head:head + 1] for part in parts], axis=0)
        attended_ref[:, head * HD:(head + 1) * HD] = both.astype(jnp.bfloat16)
    wait_guarded(guarded)


def finish(far, blocks, own, own_values, c1, c2, moved_keys, moved_values):
    moved = jax.ShapeDtypeStruct((ROWS, SPAN, WIDE), jnp.bfloat16)
    return pl.pallas_call(
        finish_kernel,
        out_shape=[jax.ShapeDtypeStruct((ROWS, QH * HD), jnp.bfloat16), moved, moved],
        in_specs=[VMEM] * 6 + [HBM] * 2,
        out_specs=[VMEM, HBM, HBM],
        input_output_aliases={6: 1, 7: 2},
        scratch_shapes=[pltpu.SemaphoreType.DMA((ROWS, 2))],
        compiler_params=pltpu.CompilerParams(vmem_limit_bytes=PART),
        cost_estimate=pl.CostEstimate(flops=2**20, bytes_accessed=2**20, transcendentals=2**16),
    )(far, blocks, own, own_values, c1, c2, moved_keys, moved_values)


def on_device(keys, values, lengths, destination, queries, new_keys, new_values):
    a1, a2, b1, b2, ask = send_buffers(destination, lengths, keys, values, queries)
    asked = lax.ppermute(ask, "x", ASK_C)
    a1 = lax.ppermute(a1, "x", EDGE_A)
    a2 = lax.ppermute(a2, "x", EDGE_A)
    b1 = lax.ppermute(b1, "x", EDGE_B)
    b2 = lax.ppermute(b2, "x", EDGE_B)
    far, own, own_values = early(destination, lengths, asked, queries, new_keys, new_values, keys, values)
    far = lax.ppermute(far, "x", EDGE_C)
    c1 = lax.ppermute(a1, "x", RELAY)
    c2 = lax.ppermute(a2, "x", RELAY)
    partial, moved_keys, moved_values = attend(destination, lengths, queries, keys, values, a1, a2, b1, b2, far)
    blocks = lax.all_to_all(partial, "t", 0, 0)
    attended, moved_keys, moved_values = finish(far, blocks, own, own_values, c1, c2, moved_keys, moved_values)
    return moved_keys, moved_values, attended


def solution(mesh):
    groups = Mesh(mesh.devices.reshape(-1, GROUP, TENSOR), ("z", "x", "t"))
    dp = ("z", "x")
    return jax.shard_map(
        on_device,
        mesh=groups,
        in_specs=(P(dp, "t", None), P(dp, "t", None), P(dp), P(dp), P(dp, None), P(dp, None), P(dp, None)),
        out_specs=(P(dp, "t", None), P(dp, "t", None), P(dp, None)),
        check_vma=False,
    )
```

```python
import functools

import jax
import jax.numpy as jnp
from jax import lax
from jax.experimental import pallas as pl
from jax.experimental.pallas import tpu as pltpu
from jax.sharding import Mesh
from jax.sharding import PartitionSpec as P

QH = 64
KVH = 8
HD = 128
SLOTS = 4
ROWS = 2
GROUP = 4
PER = QH // KVH
TENSOR = 8
SPAN = 128
WIDE = KVH * HD
SCALE = HD ** -0.5
FLOOR = -1e30

STAT = ROWS * QH
STATS = 6
PARTIAL = STAT + 16
NOTE = 16
EDGE_A = ((0, 1), (1, 0), (2, 3), (3, 2))
EDGE_B = ((1, 2), (2, 1))
EDGE_C = ((1, 3), (2, 0))
RELAY = ((0, 3), (3, 0))
ASK_C = ((3, 1), (0, 2))

CUT = 64

FULL = 60 * 2**20
PART = 16 * 2**20

SMEM = pl.BlockSpec(memory_space=pltpu.SMEM)
VMEM = pl.BlockSpec(memory_space=pltpu.VMEM)
HBM = pl.BlockSpec(memory_space=pltpu.HBM)


def replica_index():
    return lax.axis_index("x")


def first_survivor():
    return lax.axis_index("z") * (GROUP * ROWS)


def places(dest_ref, slot, first):
    local = dest_ref[slot] - first
    live = dest_ref[slot] >= 0
    return jnp.where(live, lax.shift_right_arithmetic(local, 1), -1), lax.bitwise_and(local, 1)


def along_a_pieces(row, a1_ref, a2_ref):
    if row == 0:
        return [(0, 0, SPAN, a1_ref.at[pl.ds(0, SPAN)]), (1, 0, SPAN, a1_ref.at[pl.ds(SPAN, SPAN)])]
    return [
        (0, 0, CUT, a1_ref.at[pl.ds(2 * SPAN, CUT)]),
        (0, CUT, SPAN - CUT, a2_ref.at[pl.ds(0, SPAN - CUT)]),
        (1, 0, SPAN, a2_ref.at[pl.ds(SPAN - CUT, SPAN)]),
    ]


def along_b_pieces(row, b1_ref, b2_ref):
    buffer = (b1_ref, b2_ref)[row]
    return [(0, 0, SPAN, buffer.at[pl.ds(0, SPAN)]), (1, 0, SPAN, buffer.at[pl.ds(SPAN, SPAN)])]


def send_kernel(dest_ref, length_ref, keys_ref, values_ref, queries_ref, a1_ref, a2_ref, b1_ref, b2_ref, ask_ref,
                keys, values, note, load_sem, sem, note_sem):
    first, x = first_survivor(), replica_index()
    loads = []
    for slot in range(SLOTS):
        loads.append((
            pltpu.make_async_copy(keys_ref.at[slot], keys.at[slot], load_sem.at[0, slot]),
            pltpu.make_async_copy(values_ref.at[slot], values.at[slot], load_sem.at[1, slot]),
        ))
    for pair in loads:
        for load in pair:
            load.start()
    line = lax.broadcasted_iota(jnp.int32, (NOTE, WIDE), 0)
    guarded = []
    told = [jnp.zeros((NOTE, WIDE), jnp.int32) for _ in range(2)]
    for slot in range(SLOTS):
        host, row = places(dest_ref, slot, first)
        edge = jnp.where(host >= 0, lax.bitwise_xor(host, x), -1)
        along_a = (edge == 1) | (edge == 2)
        along_b = edge == 3
        length = length_ref[slot]
        for n, along in enumerate((along_a, along_b)):
            base = jnp.where(along, row * 3, NOTE)
            for k, value in enumerate((dest_ref[slot] - first + 1, lax.shift_right_logical(length, 4), lax.bitwise_and(length, 15))):
                told[n] = jnp.where(line == base + k, value, told[n])
        for which in range(ROWS):
            mine = row == which
            for guard, parts in (
                (mine & along_a, along_a_pieces(which, a1_ref, a2_ref)),
                (mine & along_b, along_b_pieces(which, b1_ref, b2_ref)),
            ):
                guarded.append((guard, slot, [
                    pltpu.make_async_copy((keys, values)[n].at[slot].at[pl.ds(at, size)], place, sem.at[slot, i])
                    for i, (n, at, size, place) in enumerate(parts)
                ]))
    for n in range(2):
        note[n] = told[n].astype(jnp.float32).astype(jnp.bfloat16)
    notes = [
        pltpu.make_async_copy(note.at[0], a2_ref.at[pl.ds(2 * SPAN - CUT, NOTE)], note_sem.at[0]),
        pltpu.make_async_copy(note.at[1], b2_ref.at[pl.ds(2 * SPAN, NOTE)], note_sem.at[1]),
    ]
    notes.append(pltpu.make_async_copy(queries_ref, ask_ref, note_sem.at[2]))
    for copy in notes:
        copy.start()
    for slot in range(SLOTS):
        for load in loads[slot]:
            load.wait()
        start_guarded([(guard, copies) for guard, owner, copies in guarded if owner == slot])
    wait_guarded([(guard, copies) for guard, _, copies in guarded])
    for copy in notes:
        copy.wait()


def send_buffers(destination, lengths, keys, values, queries):
    buffer = lambda rows: jax.ShapeDtypeStruct((rows, WIDE), jnp.bfloat16)
    return pl.pallas_call(
        send_kernel,
        out_shape=[
            buffer(2 * SPAN + CUT), buffer(2 * SPAN - CUT + NOTE), buffer(2 * SPAN), buffer(2 * SPAN + NOTE),
            jax.ShapeDtypeStruct(queries.shape, queries.dtype),
        ],
        in_specs=[SMEM, SMEM, HBM, HBM, VMEM],
        out_specs=[HBM] * 5,
        scratch_shapes=[
            pltpu.VMEM((SLOTS, SPAN, WIDE), jnp.bfloat16),
            pltpu.VMEM((SLOTS, SPAN, WIDE), jnp.bfloat16),
            pltpu.VMEM((2, NOTE, WIDE), jnp.bfloat16),
            pltpu.SemaphoreType.DMA((2, SLOTS)),
            pltpu.SemaphoreType.DMA((SLOTS, 3)),
            pltpu.SemaphoreType.DMA((3,)),
        ],
        compiler_params=pltpu.CompilerParams(vmem_limit_bytes=FULL),
        cost_estimate=pl.CostEstimate(flops=0, bytes_accessed=4 * 2**20, transcendentals=0),
    )(destination, lengths, keys, values, queries)


def start_guarded(guarded):
    for guard, copies in guarded:
        @pl.when(guard)
        def _(copies=copies):
            for copy in copies:
                copy.start()


def wait_guarded(guarded):
    for guard, copies in guarded:
        @pl.when(guard)
        def _(copies=copies):
            for copy in copies:
                copy.wait()


def split_three(x):
    high = x.astype(jnp.bfloat16)
    rest = x - high.astype(jnp.float32)
    middle = rest.astype(jnp.bfloat16)
    low = (rest - middle.astype(jnp.float32)).astype(jnp.bfloat16)
    return high.astype(jnp.float32), middle.astype(jnp.float32), low.astype(jnp.float32)


def heads_of(ref, row):
    block = ref[...].astype(jnp.float32)
    return jnp.concatenate([block[row:row + 1, h * HD:(h + 1) * HD] for h in range(QH)], axis=0)


def spread_heads(query):
    head = lax.broadcasted_iota(jnp.int32, (QH, WIDE), 0)
    lane = lax.broadcasted_iota(jnp.int32, (QH, WIDE), 1)
    wide = jnp.concatenate([query] * KVH, axis=1)
    return jnp.where((head // PER) == (lane // HD), wide, 0.0).astype(jnp.bfloat16)


def block_attention(query, keys, values, length):
    position = lax.axis_index("t") * SPAN + lax.broadcasted_iota(jnp.int32, (QH, SPAN), 1)
    scores = lax.dot_general(
        spread_heads(query), keys, (((1,), (1,)), ((), ())), preferred_element_type=jnp.float32
    ) * SCALE
    valid = position < length
    peak = jnp.max(jnp.where(valid, scores, FLOOR), axis=1, keepdims=True)
    weights = jnp.where(valid, jnp.exp(scores - peak), 0.0).astype(jnp.bfloat16)
    mass = jnp.sum(weights.astype(jnp.float32), axis=1, keepdims=True)
    full = jnp.dot(weights, values, preferred_element_type=jnp.float32)
    partial = jnp.concatenate([full[g * PER:(g + 1) * PER, g * HD:(g + 1) * HD] for g in range(KVH)], axis=0)
    return peak, mass, partial.astype(jnp.bfloat16)


def flip(columns):
    lane = lax.broadcasted_iota(jnp.int32, (QH, HD), 1)
    block = jnp.zeros((QH, HD), jnp.float32)
    for n, column in columns.items():
        block = jnp.where(lane == n, column, block)
    return jnp.transpose(jnp.concatenate([block, jnp.zeros((HD - QH, HD), jnp.float32)], axis=0))


def statistics(row, peak, mass):
    columns = {row * STATS + k: piece for k, piece in enumerate(split_three(peak) + split_three(mass))}
    return flip(columns)[:16].astype(jnp.bfloat16)


def mine(row):
    line = lax.broadcasted_iota(jnp.int32, (16, HD), 0)
    return (line >= row * STATS) & (line < (row + 1) * STATS)


def early_kernel(dest_ref, length_ref, asked_ref, queries_ref, new_keys_ref, new_values_ref, keys_ref, values_ref,
                 far_ref, own_ref, own_values_ref, keys, values, sem):
    first, x = first_survivor(), replica_index()
    line = lax.broadcasted_iota(jnp.int32, (NOTE, HD), 0)
    told = jnp.zeros((NOTE, HD), jnp.int32)
    far = []
    guarded = []
    for row in range(ROWS):
        found, length = jnp.int32(-1), jnp.int32(0)
        wanted = lax.bitwise_xor(x, 2) * ROWS + row + first
        for slot in range(SLOTS):
            hit = dest_ref[slot] == wanted
            found = jnp.where(hit, slot, found)
            length = jnp.where(hit, length_ref[slot], length)
        told = jnp.where((line == row * 3) & (found >= 0), wanted - first + 1, told)
        slot = jnp.maximum(found, 0)
        guarded.append((found >= 0, [
            pltpu.make_async_copy(keys_ref.at[slot], keys.at[row], sem.at[row, 0]),
            pltpu.make_async_copy(values_ref.at[slot], values.at[row], sem.at[row, 1]),
        ]))
        far.append((found, length))
    start_guarded(guarded)
    far_ref[PARTIAL:, :] = told.astype(jnp.float32).astype(jnp.bfloat16)
    far_ref[STAT:PARTIAL, :] = jnp.zeros((16, HD), jnp.bfloat16)
    own = {}
    for row in range(ROWS):
        def per_head(ref):
            block = ref[...].astype(jnp.float32)
            return jnp.concatenate([
                jnp.broadcast_to(block[row:row + 1, g * HD:(g + 1) * HD], (PER, HD)) for g in range(KVH)
            ], axis=0)

        own[row] = jnp.sum(heads_of(queries_ref, row) * per_head(new_keys_ref), axis=1, keepdims=True) * SCALE
        own_values_ref[row] = per_head(new_values_ref)
    own_ref[...] = flip(own)[:8]
    wait_guarded(guarded)
    for row, (found, length) in enumerate(far):
        @pl.when(found >= 0)
        def _(row=row, length=length):
            peak, mass, partial = block_attention(heads_of(asked_ref, row), keys[row], values[row], length)
            far_ref[row * QH:(row + 1) * QH, :] = partial
            far_ref[STAT:PARTIAL, :] = jnp.where(mine(row), statistics(row, peak, mass), far_ref[STAT:PARTIAL, :])


def early(destination, lengths, asked, queries, new_keys, new_values, keys, values):
    return pl.pallas_call(
        early_kernel,
        out_shape=[
            jax.ShapeDtypeStruct((PARTIAL + NOTE, HD), jnp.bfloat16),
            jax.ShapeDtypeStruct((8, HD), jnp.float32),
            jax.ShapeDtypeStruct((ROWS, QH, HD), jnp.float32),
        ],
        in_specs=[SMEM, SMEM] + [VMEM] * 4 + [HBM] * 2,
        out_specs=[VMEM] * 3,
        scratch_shapes=[
            pltpu.VMEM((ROWS, SPAN, WIDE), jnp.bfloat16),
            pltpu.VMEM((ROWS, SPAN, WIDE), jnp.bfloat16),
            pltpu.SemaphoreType.DMA((ROWS, 2)),
        ],
        compiler_params=pltpu.CompilerParams(vmem_limit_bytes=PART),
        cost_estimate=pl.CostEstimate(flops=2**32, bytes_accessed=2**20, transcendentals=2**14),
    )(destination, lengths, asked, queries, new_keys, new_values, keys, values)


def attend_kernel(dest_ref, length_ref, queries_ref, keys_ref, values_ref, a1_ref, a2_ref, b1_ref, b2_ref, far_ref,
                  out_ref, moved_keys_ref, moved_values_ref, stage, pack, sem, moved_sem):
    first, x = first_survivor(), replica_index()
    note_a = a2_ref[2 * SPAN - CUT:, :HD].astype(jnp.float32)
    note_b = b2_ref[2 * SPAN:, :HD].astype(jnp.float32)
    line = lax.broadcasted_iota(jnp.int32, (NOTE, HD), 0)
    rows = []
    guarded = []
    for row in range(ROWS):
        wanted = x * ROWS + row
        here, slot, length = jnp.bool_(False), jnp.int32(0), jnp.int32(0)
        for k in range(SLOTS):
            hit = dest_ref[k] == wanted + first
            here = here | hit
            slot = jnp.where(hit, k, slot)
            length = jnp.where(hit, length_ref[k], length)

        def read(note, k):
            return jnp.max(jnp.where(line == row * 3 + k, note, 0.0)).astype(jnp.int32)

        in_a, in_b = read(note_a, 0) == wanted + 1, read(note_b, 0) == wanted + 1
        length = jnp.where(in_a, read(note_a, 1) * 16 + read(note_a, 2), length)
        length = jnp.where(in_b, read(note_b, 1) * 16 + read(note_b, 2), length)
        rows.append((here | in_a | in_b, length))
        base = 2 * SPAN * row
        for guard, parts in (
            (here, [(0, 0, SPAN, keys_ref.at[slot]), (1, 0, SPAN, values_ref.at[slot])]),
            (in_a, along_a_pieces(row, a1_ref, a2_ref)),
            (in_b, along_b_pieces(row, b1_ref, b2_ref)),
        ):
            guarded.append((guard, [
                pltpu.make_async_copy(place, stage.at[pl.ds(base + n * SPAN + at, size)], sem.at[row, i])
                for i, (n, at, size, place) in enumerate(parts)
            ]))
    start_guarded(guarded)
    pack[...] = far_ref[:PARTIAL, :]
    wait_guarded(guarded)
    moves = []
    for row, (near, _) in enumerate(rows):
        base = 2 * SPAN * row
        moves.append((near, [
            pltpu.make_async_copy(stage.at[pl.ds(base, SPAN)], moved_keys_ref.at[row], moved_sem.at[row, 0]),
            pltpu.make_async_copy(stage.at[pl.ds(base + SPAN, SPAN)], moved_values_ref.at[row], moved_sem.at[row, 1]),
        ]))
    start_guarded(moves)
    results = [
        block_attention(
            heads_of(queries_ref, row), stage[2 * SPAN * row:2 * SPAN * row + SPAN],
            stage[2 * SPAN * row + SPAN:2 * SPAN * (row + 1)], length,
        )
        for row, (_, length) in enumerate(rows)
    ]
    for row, ((near, _), (peak, mass, partial)) in enumerate(zip(rows, results)):
        @pl.when(near)
        def _(row=row, peak=peak, mass=mass, partial=partial):
            pack[row * QH:(row + 1) * QH, :] = partial
            pack[STAT:PARTIAL, :] = jnp.where(mine(row), statistics(row, peak, mass), pack[STAT:PARTIAL, :])
    for peer in range(TENSOR):
        out_ref[peer] = pack[...]
    wait_guarded(moves)


def attend(destination, lengths, queries, keys, values, a1, a2, b1, b2, far):
    moved = jax.ShapeDtypeStruct((ROWS, SPAN, WIDE), jnp.bfloat16)
    return pl.pallas_call(
        attend_kernel,
        out_shape=[jax.ShapeDtypeStruct((TENSOR, PARTIAL, HD), jnp.bfloat16), moved, moved],
        in_specs=[SMEM, SMEM, VMEM, HBM, HBM, HBM, VMEM, HBM, VMEM, VMEM],
        out_specs=[VMEM, HBM, HBM],
        scratch_shapes=[
            pltpu.VMEM((4 * SPAN, WIDE), jnp.bfloat16),
            pltpu.VMEM((PARTIAL, HD), jnp.bfloat16),
            pltpu.SemaphoreType.DMA((ROWS, 3)),
            pltpu.SemaphoreType.DMA((ROWS, 2)),
        ],
        compiler_params=pltpu.CompilerParams(vmem_limit_bytes=PART),
        cost_estimate=pl.CostEstimate(flops=2**31, bytes_accessed=2 * 2**20, transcendentals=2**14),
    )(destination, lengths, queries, keys, values, a1, a2, b1, b2, far)


def finish_kernel(far_ref, blocks_ref, own_ref, own_values_ref, c1_ref, c2_ref, keys_in_ref, values_in_ref,
                  attended_ref, moved_keys_ref, moved_values_ref, sem):
    x = replica_index()
    note = far_ref[PARTIAL:, :].astype(jnp.float32)
    line = lax.broadcasted_iota(jnp.int32, (NOTE, HD), 0)
    guarded = []
    for row in range(ROWS):
        told = jnp.max(jnp.where(line == row * 3, note, 0.0)).astype(jnp.int32)
        guarded.append((told == x * ROWS + row + 1, [
            pltpu.make_async_copy(place, (moved_keys_ref, moved_values_ref)[n].at[row].at[pl.ds(at, size)], sem.at[row, i])
            for i, (n, at, size, place) in enumerate(along_a_pieces(row, c1_ref, c2_ref))
        ]))
    start_guarded(guarded)
    stats = [blocks_ref[b, STAT:PARTIAL, :].astype(jnp.float32) for b in range(TENSOR)]
    columns = []
    for row in range(ROWS):
        at = row * STATS
        peaks = [(one[at:at + 1] + one[at + 1:at + 2]) + one[at + 2:at + 3] for one in stats]
        masses = [(one[at + 3:at + 4] + one[at + 4:at + 5]) + one[at + 5:at + 6] for one in stats]
        own = own_ref[row:row + 1, :]
        top = functools.reduce(jnp.maximum, peaks, own)
        fades = [jnp.exp(peak - top) for peak in peaks]
        own_weight = jnp.exp(own - top)
        denominator = own_weight
        for fade, mass in zip(fades, masses):
            denominator = denominator + fade * mass
        columns += [one / denominator for one in fades + [own_weight]]
    columns.append(jnp.zeros((HD - len(columns), HD), jnp.float32))
    shares = jnp.transpose(jnp.concatenate(columns, axis=0))[:QH]
    parts = []
    for row in range(ROWS):
        at = row * (TENSOR + 1)
        total = shares[:, at + TENSOR:at + TENSOR + 1] * own_values_ref[row]
        for b in range(TENSOR):
            total = total + shares[:, at + b:at + b + 1] * blocks_ref[b, row * QH:(row + 1) * QH, :].astype(jnp.float32)
        parts.append(total)
    for head in range(QH):
        both = jnp.concatenate([part[head:head + 1] for part in parts], axis=0)
        attended_ref[:, head * HD:(head + 1) * HD] = both.astype(jnp.bfloat16)
    wait_guarded(guarded)


def finish(far, blocks, own, own_values, c1, c2, moved_keys, moved_values):
    moved = jax.ShapeDtypeStruct((ROWS, SPAN, WIDE), jnp.bfloat16)
    return pl.pallas_call(
        finish_kernel,
        out_shape=[jax.ShapeDtypeStruct((ROWS, QH * HD), jnp.bfloat16), moved, moved],
        in_specs=[VMEM] * 6 + [HBM] * 2,
        out_specs=[VMEM, HBM, HBM],
        input_output_aliases={6: 1, 7: 2},
        scratch_shapes=[pltpu.SemaphoreType.DMA((ROWS, 3))],
        compiler_params=pltpu.CompilerParams(vmem_limit_bytes=PART),
        cost_estimate=pl.CostEstimate(flops=2**20, bytes_accessed=2**20, transcendentals=2**16),
    )(far, blocks, own, own_values, c1, c2, moved_keys, moved_values)


def on_device(keys, values, lengths, destination, queries, new_keys, new_values):
    a1, a2, b1, b2, ask = send_buffers(destination, lengths, keys, values, queries)
    asked = lax.ppermute(ask, "x", ASK_C)
    a1 = lax.ppermute(a1, "x", EDGE_A)
    a2 = lax.ppermute(a2, "x", EDGE_A)
    b1 = lax.ppermute(b1, "x", EDGE_B)
    b2 = lax.ppermute(b2, "x", EDGE_B)
    far, own, own_values = early(destination, lengths, asked, queries, new_keys, new_values, keys, values)
    far = lax.ppermute(far, "x", EDGE_C)
    c1 = lax.ppermute(a1, "x", RELAY)
    c2 = lax.ppermute(a2, "x", RELAY)
    partial, moved_keys, moved_values = attend(destination, lengths, queries, keys, values, a1, a2, b1, b2, far)
    blocks = lax.all_to_all(partial, "t", 0, 0)
    attended, moved_keys, moved_values = finish(far, blocks, own, own_values, c1, c2, moved_keys, moved_values)
    return moved_keys, moved_values, attended


def solution(mesh):
    groups = Mesh(mesh.devices.reshape(-1, GROUP, TENSOR), ("z", "x", "t"))
    dp = ("z", "x")
    return jax.shard_map(
        on_device,
        mesh=groups,
        in_specs=(P(dp, "t", None), P(dp, "t", None), P(dp), P(dp), P(dp, None), P(dp, None), P(dp, None)),
        out_specs=(P(dp, "t", None), P(dp, "t", None), P(dp, None)),
        check_vma=False,
    )
```

```python
import functools

import jax
import jax.numpy as jnp
from jax import lax
from jax.experimental import pallas as pl
from jax.experimental.pallas import tpu as pltpu
from jax.sharding import Mesh
from jax.sharding import PartitionSpec as P

QH = 64
KVH = 8
HD = 128
SLOTS = 4
ROWS = 2
GROUP = 4
PER = QH // KVH
TENSOR = 8
SPAN = 128
WIDE = KVH * HD
SCALE = HD ** -0.5
FLOOR = -1e30

STAT = ROWS * QH
STATS = 6
PARTIAL = STAT + 16
NOTE = 16
EDGE_A = ((0, 1), (1, 0), (2, 3), (3, 2))
EDGE_B = ((1, 2), (2, 1))
EDGE_C = ((1, 3), (2, 0))
RELAY = ((0, 3), (3, 0))
ASK_C = ((3, 1), (0, 2))

CUT = 64

FULL = 60 * 2**20
PART = 16 * 2**20

SMEM = pl.BlockSpec(memory_space=pltpu.SMEM)
VMEM = pl.BlockSpec(memory_space=pltpu.VMEM)
HBM = pl.BlockSpec(memory_space=pltpu.HBM)


def replica_index():
    return lax.axis_index("x")


def first_survivor():
    return lax.axis_index("z") * (GROUP * ROWS)


def places(dest_ref, slot, first):
    local = dest_ref[slot] - first
    live = dest_ref[slot] >= 0
    return jnp.where(live, lax.shift_right_arithmetic(local, 1), -1), lax.bitwise_and(local, 1)


def along_a_pieces(row, a1_ref, a2_ref):
    if row == 0:
        return [(0, 0, SPAN, a1_ref.at[pl.ds(0, SPAN)]), (1, 0, SPAN, a1_ref.at[pl.ds(SPAN, SPAN)])]
    return [
        (0, 0, CUT, a1_ref.at[pl.ds(2 * SPAN, CUT)]),
        (0, CUT, SPAN - CUT, a2_ref.at[pl.ds(0, SPAN - CUT)]),
        (1, 0, SPAN, a2_ref.at[pl.ds(SPAN - CUT, SPAN)]),
    ]


def along_b_pieces(row, b1_ref, b2_ref):
    buffer = (b1_ref, b2_ref)[row]
    return [(0, 0, SPAN, buffer.at[pl.ds(0, SPAN)]), (1, 0, SPAN, buffer.at[pl.ds(SPAN, SPAN)])]


def send_kernel(dest_ref, length_ref, keys_ref, values_ref, queries_ref, a1_ref, a2_ref, b1_ref, b2_ref, ask_ref,
                keys, values, note, load_sem, sem, note_sem):
    first, x = first_survivor(), replica_index()
    loads = []
    for slot in range(SLOTS):
        loads.append((
            pltpu.make_async_copy(keys_ref.at[slot], keys.at[slot], load_sem.at[0, slot]),
            pltpu.make_async_copy(values_ref.at[slot], values.at[slot], load_sem.at[1, slot]),
        ))
    for pair in loads:
        for load in pair:
            load.start()
    line = lax.broadcasted_iota(jnp.int32, (NOTE, WIDE), 0)
    guarded = []
    told = [jnp.zeros((NOTE, WIDE), jnp.int32) for _ in range(2)]
    for slot in range(SLOTS):
        host, row = places(dest_ref, slot, first)
        edge = jnp.where(host >= 0, lax.bitwise_xor(host, x), -1)
        along_a = (edge == 1) | (edge == 2)
        along_b = edge == 3
        length = length_ref[slot]
        for n, along in enumerate((along_a, along_b)):
            base = jnp.where(along, row * 3, NOTE)
            for k, value in enumerate((dest_ref[slot] - first + 1, lax.shift_right_logical(length, 4), lax.bitwise_and(length, 15))):
                told[n] = jnp.where(line == base + k, value, told[n])
        for which in range(ROWS):
            mine = row == which
            for guard, parts in (
                (mine & along_a, along_a_pieces(which, a1_ref, a2_ref)),
                (mine & along_b, along_b_pieces(which, b1_ref, b2_ref)),
            ):
                guarded.append((guard, slot, [
                    pltpu.make_async_copy((keys, values)[n].at[slot].at[pl.ds(at, size)], place, sem.at[slot, i])
                    for i, (n, at, size, place) in enumerate(parts)
                ]))
    for n in range(2):
        note[n] = told[n].astype(jnp.float32).astype(jnp.bfloat16)
    notes = [
        pltpu.make_async_copy(note.at[0], a2_ref.at[pl.ds(2 * SPAN - CUT, NOTE)], note_sem.at[0]),
        pltpu.make_async_copy(note.at[1], b2_ref.at[pl.ds(2 * SPAN, NOTE)], note_sem.at[1]),
    ]
    notes.append(pltpu.make_async_copy(queries_ref, ask_ref, note_sem.at[2]))
    for copy in notes:
        copy.start()
    for slot in range(SLOTS):
        for load in loads[slot]:
            load.wait()
        start_guarded([(guard, copies) for guard, owner, copies in guarded if owner == slot])
    wait_guarded([(guard, copies) for guard, _, copies in guarded])
    for copy in notes:
        copy.wait()


def send_buffers(destination, lengths, keys, values, queries):
    buffer = lambda rows: jax.ShapeDtypeStruct((rows, WIDE), jnp.bfloat16)
    return pl.pallas_call(
        send_kernel,
        out_shape=[
            buffer(2 * SPAN + CUT), buffer(2 * SPAN - CUT + NOTE), buffer(2 * SPAN), buffer(2 * SPAN + NOTE),
            jax.ShapeDtypeStruct(queries.shape, queries.dtype),
        ],
        in_specs=[SMEM, SMEM, HBM, HBM, VMEM],
        out_specs=[HBM] * 5,
        scratch_shapes=[
            pltpu.VMEM((SLOTS, SPAN, WIDE), jnp.bfloat16),
            pltpu.VMEM((SLOTS, SPAN, WIDE), jnp.bfloat16),
            pltpu.VMEM((2, NOTE, WIDE), jnp.bfloat16),
            pltpu.SemaphoreType.DMA((2, SLOTS)),
            pltpu.SemaphoreType.DMA((SLOTS, 3)),
            pltpu.SemaphoreType.DMA((3,)),
        ],
        compiler_params=pltpu.CompilerParams(vmem_limit_bytes=FULL),
        cost_estimate=pl.CostEstimate(flops=0, bytes_accessed=4 * 2**20, transcendentals=0),
    )(destination, lengths, keys, values, queries)


def start_guarded(guarded):
    for guard, copies in guarded:
        @pl.when(guard)
        def _(copies=copies):
            for copy in copies:
                copy.start()


def wait_guarded(guarded):
    for guard, copies in guarded:
        @pl.when(guard)
        def _(copies=copies):
            for copy in copies:
                copy.wait()


def split_three(x):
    high = x.astype(jnp.bfloat16)
    rest = x - high.astype(jnp.float32)
    middle = rest.astype(jnp.bfloat16)
    low = (rest - middle.astype(jnp.float32)).astype(jnp.bfloat16)
    return high.astype(jnp.float32), middle.astype(jnp.float32), low.astype(jnp.float32)


def heads_of(ref, row):
    block = ref[...].astype(jnp.float32)
    return jnp.concatenate([block[row:row + 1, h * HD:(h + 1) * HD] for h in range(QH)], axis=0)


def spread_heads(query):
    head = lax.broadcasted_iota(jnp.int32, (QH, WIDE), 0)
    lane = lax.broadcasted_iota(jnp.int32, (QH, WIDE), 1)
    wide = jnp.concatenate([query] * KVH, axis=1)
    return jnp.where((head // PER) == (lane // HD), wide, 0.0).astype(jnp.bfloat16)


def block_attention(spread, keys, values, length):
    position = lax.axis_index("t") * SPAN + lax.broadcasted_iota(jnp.int32, (QH, SPAN), 1)
    scores = lax.dot_general(
        spread, keys, (((1,), (1,)), ((), ())), preferred_element_type=jnp.float32
    ) * SCALE
    valid = position < length
    peak = jnp.max(jnp.where(valid, scores, FLOOR), axis=1, keepdims=True)
    weights = jnp.where(valid, jnp.exp(scores - peak), 0.0).astype(jnp.bfloat16)
    mass = jnp.sum(weights.astype(jnp.float32), axis=1, keepdims=True)
    full = jnp.dot(weights, values, preferred_element_type=jnp.float32)
    partial = jnp.concatenate([full[g * PER:(g + 1) * PER, g * HD:(g + 1) * HD] for g in range(KVH)], axis=0)
    return peak, mass, partial.astype(jnp.bfloat16)


def flip(columns):
    lane = lax.broadcasted_iota(jnp.int32, (QH, HD), 1)
    block = jnp.zeros((QH, HD), jnp.float32)
    for n, column in columns.items():
        block = jnp.where(lane == n, column, block)
    return jnp.transpose(jnp.concatenate([block, jnp.zeros((HD - QH, HD), jnp.float32)], axis=0))


def statistics(row, peak, mass):
    columns = {row * STATS + k: piece for k, piece in enumerate(split_three(peak) + split_three(mass))}
    return flip(columns)[:16].astype(jnp.bfloat16)


def mine(row):
    line = lax.broadcasted_iota(jnp.int32, (16, HD), 0)
    return (line >= row * STATS) & (line < (row + 1) * STATS)


def early_kernel(dest_ref, length_ref, asked_ref, queries_ref, new_keys_ref, new_values_ref, keys_ref, values_ref,
                 far_ref, own_ref, own_values_ref, keys, values, sem):
    first, x = first_survivor(), replica_index()
    line = lax.broadcasted_iota(jnp.int32, (NOTE, HD), 0)
    told = jnp.zeros((NOTE, HD), jnp.int32)
    far = []
    guarded = []
    for row in range(ROWS):
        found, length = jnp.int32(-1), jnp.int32(0)
        wanted = lax.bitwise_xor(x, 2) * ROWS + row + first
        for slot in range(SLOTS):
            hit = dest_ref[slot] == wanted
            found = jnp.where(hit, slot, found)
            length = jnp.where(hit, length_ref[slot], length)
        told = jnp.where((line == row * 3) & (found >= 0), wanted - first + 1, told)
        slot = jnp.maximum(found, 0)
        guarded.append((found >= 0, [
            pltpu.make_async_copy(keys_ref.at[slot], keys.at[row], sem.at[row, 0]),
            pltpu.make_async_copy(values_ref.at[slot], values.at[row], sem.at[row, 1]),
        ]))
        far.append((found, length))
    start_guarded(guarded)
    far_ref[PARTIAL:, :] = told.astype(jnp.float32).astype(jnp.bfloat16)
    far_ref[STAT:PARTIAL, :] = jnp.zeros((16, HD), jnp.bfloat16)
    own = {}
    for row in range(ROWS):
        def per_head(ref):
            block = ref[...].astype(jnp.float32)
            return jnp.concatenate([
                jnp.broadcast_to(block[row:row + 1, g * HD:(g + 1) * HD], (PER, HD)) for g in range(KVH)
            ], axis=0)

        own[row] = jnp.sum(heads_of(queries_ref, row) * per_head(new_keys_ref), axis=1, keepdims=True) * SCALE
        own_values_ref[row] = per_head(new_values_ref)
    own_ref[...] = flip(own)[:8]
    wait_guarded(guarded)
    for row, (found, length) in enumerate(far):
        @pl.when(found >= 0)
        def _(row=row, length=length):
            peak, mass, partial = block_attention(spread_heads(heads_of(asked_ref, row)), keys[row], values[row], length)
            far_ref[row * QH:(row + 1) * QH, :] = partial
            far_ref[STAT:PARTIAL, :] = jnp.where(mine(row), statistics(row, peak, mass), far_ref[STAT:PARTIAL, :])


def early(destination, lengths, asked, queries, new_keys, new_values, keys, values):
    return pl.pallas_call(
        early_kernel,
        out_shape=[
            jax.ShapeDtypeStruct((PARTIAL + NOTE, HD), jnp.bfloat16),
            jax.ShapeDtypeStruct((8, HD), jnp.float32),
            jax.ShapeDtypeStruct((ROWS, QH, HD), jnp.float32),
        ],
        in_specs=[SMEM, SMEM] + [VMEM] * 4 + [HBM] * 2,
        out_specs=[VMEM] * 3,
        scratch_shapes=[
            pltpu.VMEM((ROWS, SPAN, WIDE), jnp.bfloat16),
            pltpu.VMEM((ROWS, SPAN, WIDE), jnp.bfloat16),
            pltpu.SemaphoreType.DMA((ROWS, 2)),
        ],
        compiler_params=pltpu.CompilerParams(vmem_limit_bytes=PART),
        cost_estimate=pl.CostEstimate(flops=2**32, bytes_accessed=2**20, transcendentals=2**14),
    )(destination, lengths, asked, queries, new_keys, new_values, keys, values)


def attend_kernel(dest_ref, length_ref, queries_ref, keys_ref, values_ref, a1_ref, a2_ref, b1_ref, b2_ref, far_ref,
                  out_ref, moved_keys_ref, moved_values_ref, stage, pack, spread, sem, moved_sem):
    first, x = first_survivor(), replica_index()
    note_a = a2_ref[2 * SPAN - CUT:, :HD].astype(jnp.float32)
    note_b = b2_ref[2 * SPAN:, :HD].astype(jnp.float32)
    line = lax.broadcasted_iota(jnp.int32, (NOTE, HD), 0)
    rows = []
    guarded = []
    for row in range(ROWS):
        wanted = x * ROWS + row
        here, slot, length = jnp.bool_(False), jnp.int32(0), jnp.int32(0)
        for k in range(SLOTS):
            hit = dest_ref[k] == wanted + first
            here = here | hit
            slot = jnp.where(hit, k, slot)
            length = jnp.where(hit, length_ref[k], length)

        def read(note, k):
            return jnp.max(jnp.where(line == row * 3 + k, note, 0.0)).astype(jnp.int32)

        in_a, in_b = read(note_a, 0) == wanted + 1, read(note_b, 0) == wanted + 1
        length = jnp.where(in_a, read(note_a, 1) * 16 + read(note_a, 2), length)
        length = jnp.where(in_b, read(note_b, 1) * 16 + read(note_b, 2), length)
        rows.append((here | in_a | in_b, length))
        base = 2 * SPAN * row
        for guard, parts in (
            (here, [(0, 0, SPAN, keys_ref.at[slot]), (1, 0, SPAN, values_ref.at[slot])]),
            (in_a, along_a_pieces(row, a1_ref, a2_ref)),
            (in_b, along_b_pieces(row, b1_ref, b2_ref)),
        ):
            guarded.append((guard, [
                pltpu.make_async_copy(place, stage.at[pl.ds(base + n * SPAN + at, size)], sem.at[row, i])
                for i, (n, at, size, place) in enumerate(parts)
            ]))
    start_guarded(guarded)
    pack[...] = far_ref[:PARTIAL, :]
    for row in range(ROWS):
        spread[row] = spread_heads(heads_of(queries_ref, row))
    wait_guarded(guarded)
    moves = []
    for row, (near, _) in enumerate(rows):
        base = 2 * SPAN * row
        moves.append((near, [
            pltpu.make_async_copy(stage.at[pl.ds(base, SPAN)], moved_keys_ref.at[row], moved_sem.at[row, 0]),
            pltpu.make_async_copy(stage.at[pl.ds(base + SPAN, SPAN)], moved_values_ref.at[row], moved_sem.at[row, 1]),
        ]))
    start_guarded(moves)
    results = [
        block_attention(
            spread[row], stage[2 * SPAN * row:2 * SPAN * row + SPAN],
            stage[2 * SPAN * row + SPAN:2 * SPAN * (row + 1)], length,
        )
        for row, (_, length) in enumerate(rows)
    ]
    for row, ((near, _), (peak, mass, partial)) in enumerate(zip(rows, results)):
        @pl.when(near)
        def _(row=row, peak=peak, mass=mass, partial=partial):
            pack[row * QH:(row + 1) * QH, :] = partial
            pack[STAT:PARTIAL, :] = jnp.where(mine(row), statistics(row, peak, mass), pack[STAT:PARTIAL, :])
    for peer in range(TENSOR):
        out_ref[peer] = pack[...]
    wait_guarded(moves)


def attend(destination, lengths, queries, keys, values, a1, a2, b1, b2, far):
    moved = jax.ShapeDtypeStruct((ROWS, SPAN, WIDE), jnp.bfloat16)
    return pl.pallas_call(
        attend_kernel,
        out_shape=[jax.ShapeDtypeStruct((TENSOR, PARTIAL, HD), jnp.bfloat16), moved, moved],
        in_specs=[SMEM, SMEM, VMEM, HBM, HBM, HBM, VMEM, HBM, VMEM, VMEM],
        out_specs=[VMEM, HBM, HBM],
        scratch_shapes=[
            pltpu.VMEM((4 * SPAN, WIDE), jnp.bfloat16),
            pltpu.VMEM((PARTIAL, HD), jnp.bfloat16),
            pltpu.VMEM((ROWS, QH, WIDE), jnp.bfloat16),
            pltpu.SemaphoreType.DMA((ROWS, 3)),
            pltpu.SemaphoreType.DMA((ROWS, 2)),
        ],
        compiler_params=pltpu.CompilerParams(vmem_limit_bytes=PART),
        cost_estimate=pl.CostEstimate(flops=2**31, bytes_accessed=2 * 2**20, transcendentals=2**14),
    )(destination, lengths, queries, keys, values, a1, a2, b1, b2, far)


def relayed_kernel(far_ref, c1_ref, c2_ref, keys_in_ref, values_in_ref, moved_keys_ref, moved_values_ref, sem):
    x = replica_index()
    note = far_ref[PARTIAL:, :].astype(jnp.float32)
    line = lax.broadcasted_iota(jnp.int32, (NOTE, HD), 0)
    guarded = []
    for row in range(ROWS):
        told = jnp.max(jnp.where(line == row * 3, note, 0.0)).astype(jnp.int32)
        guarded.append((told == x * ROWS + row + 1, [
            pltpu.make_async_copy(place, (moved_keys_ref, moved_values_ref)[n].at[row].at[pl.ds(at, size)], sem.at[row, i])
            for i, (n, at, size, place) in enumerate(along_a_pieces(row, c1_ref, c2_ref))
        ]))
    start_guarded(guarded)
    wait_guarded(guarded)


def place_relayed(far, c1, c2, moved_keys, moved_values):
    moved = jax.ShapeDtypeStruct((ROWS, SPAN, WIDE), jnp.bfloat16)
    return pl.pallas_call(
        relayed_kernel,
        out_shape=[moved, moved],
        in_specs=[VMEM] * 3 + [HBM] * 2,
        out_specs=[HBM, HBM],
        input_output_aliases={3: 0, 4: 1},
        scratch_shapes=[pltpu.SemaphoreType.DMA((ROWS, 3))],
        compiler_params=pltpu.CompilerParams(vmem_limit_bytes=PART),
        cost_estimate=pl.CostEstimate(flops=0, bytes_accessed=2**20, transcendentals=0),
    )(far, c1, c2, moved_keys, moved_values)


def finish_kernel(blocks_ref, own_ref, own_values_ref, attended_ref):
    stats = [blocks_ref[b, STAT:PARTIAL, :].astype(jnp.float32) for b in range(TENSOR)]
    columns = []
    for row in range(ROWS):
        at = row * STATS
        peaks = [(one[at:at + 1] + one[at + 1:at + 2]) + one[at + 2:at + 3] for one in stats]
        masses = [(one[at + 3:at + 4] + one[at + 4:at + 5]) + one[at + 5:at + 6] for one in stats]
        own = own_ref[row:row + 1, :]
        top = functools.reduce(jnp.maximum, peaks, own)
        fades = [jnp.exp(peak - top) for peak in peaks]
        own_weight = jnp.exp(own - top)
        denominator = own_weight
        for fade, mass in zip(fades, masses):
            denominator = denominator + fade * mass
        columns += [one / denominator for one in fades + [own_weight]]
    columns.append(jnp.zeros((HD - len(columns), HD), jnp.float32))
    shares = jnp.transpose(jnp.concatenate(columns, axis=0))[:QH]
    parts = []
    for row in range(ROWS):
        at = row * (TENSOR + 1)
        total = shares[:, at + TENSOR:at + TENSOR + 1] * own_values_ref[row]
        for b in range(TENSOR):
            total = total + shares[:, at + b:at + b + 1] * blocks_ref[b, row * QH:(row + 1) * QH, :].astype(jnp.float32)
        parts.append(total)
    for head in range(QH):
        both = jnp.concatenate([part[head:head + 1] for part in parts], axis=0)
        attended_ref[:, head * HD:(head + 1) * HD] = both.astype(jnp.bfloat16)


def finish(blocks, own, own_values):
    return pl.pallas_call(
        finish_kernel,
        out_shape=jax.ShapeDtypeStruct((ROWS, QH * HD), jnp.bfloat16),
        in_specs=[VMEM] * 3,
        out_specs=VMEM,
        compiler_params=pltpu.CompilerParams(vmem_limit_bytes=PART),
        cost_estimate=pl.CostEstimate(flops=2**20, bytes_accessed=2**20, transcendentals=2**16),
    )(blocks, own, own_values)


def on_device(keys, values, lengths, destination, queries, new_keys, new_values):
    a1, a2, b1, b2, ask = send_buffers(destination, lengths, keys, values, queries)
    asked = lax.ppermute(ask, "x", ASK_C)
    a1 = lax.ppermute(a1, "x", EDGE_A)
    a2 = lax.ppermute(a2, "x", EDGE_A)
    b1 = lax.ppermute(b1, "x", EDGE_B)
    b2 = lax.ppermute(b2, "x", EDGE_B)
    far, own, own_values = early(destination, lengths, asked, queries, new_keys, new_values, keys, values)
    far = lax.ppermute(far, "x", EDGE_C)
    c1 = lax.ppermute(a1, "x", RELAY)
    c2 = lax.ppermute(a2, "x", RELAY)
    partial, moved_keys, moved_values = attend(destination, lengths, queries, keys, values, a1, a2, b1, b2, far)
    blocks = lax.all_to_all(partial, "t", 0, 0)
    moved_keys, moved_values = place_relayed(far, c1, c2, moved_keys, moved_values)
    attended = finish(blocks, own, own_values)
    return moved_keys, moved_values, attended


def solution(mesh):
    groups = Mesh(mesh.devices.reshape(-1, GROUP, TENSOR), ("z", "x", "t"))
    dp = ("z", "x")
    return jax.shard_map(
        on_device,
        mesh=groups,
        in_specs=(P(dp, "t", None), P(dp, "t", None), P(dp), P(dp), P(dp, None), P(dp, None), P(dp, None)),
        out_specs=(P(dp, "t", None), P(dp, "t", None), P(dp, None)),
        check_vma=False,
    )
```

```python
import functools

import jax
import jax.numpy as jnp
from jax import lax
from jax.experimental import pallas as pl
from jax.experimental.pallas import tpu as pltpu
from jax.sharding import Mesh
from jax.sharding import PartitionSpec as P

QH = 64
KVH = 8
HD = 128
SLOTS = 4
ROWS = 2
GROUP = 4
PER = QH // KVH
TENSOR = 8
SPAN = 128
WIDE = KVH * HD
SCALE = HD ** -0.5
FLOOR = -1e30

STAT = ROWS * QH
STATS = 6
PARTIAL = STAT + 16
NOTE = 16
EDGE_A = ((0, 1), (1, 0), (2, 3), (3, 2))
EDGE_B = ((1, 2), (2, 1))
EDGE_C = ((1, 3), (2, 0))
RELAY = ((0, 3), (3, 0))
ASK_C = ((3, 1), (0, 2))

CUT = 64

FULL = 60 * 2**20
PART = 16 * 2**20

SMEM = pl.BlockSpec(memory_space=pltpu.SMEM)
VMEM = pl.BlockSpec(memory_space=pltpu.VMEM)
HBM = pl.BlockSpec(memory_space=pltpu.HBM)


def replica_index():
    return lax.axis_index("x")


def first_survivor():
    return lax.axis_index("z") * (GROUP * ROWS)


def places(dest_ref, slot, first):
    local = dest_ref[slot] - first
    live = dest_ref[slot] >= 0
    return jnp.where(live, lax.shift_right_arithmetic(local, 1), -1), lax.bitwise_and(local, 1)


def along_a_pieces(row, a1_ref, a2_ref):
    if row == 0:
        return [(0, 0, SPAN, a1_ref.at[pl.ds(0, SPAN)]), (1, 0, SPAN, a1_ref.at[pl.ds(SPAN, SPAN)])]
    return [
        (0, 0, CUT, a1_ref.at[pl.ds(2 * SPAN, CUT)]),
        (0, CUT, SPAN - CUT, a2_ref.at[pl.ds(0, SPAN - CUT)]),
        (1, 0, SPAN, a2_ref.at[pl.ds(SPAN - CUT, SPAN)]),
    ]


def along_b_pieces(row, b1_ref, b2_ref):
    buffer = (b1_ref, b2_ref)[row]
    return [(0, 0, SPAN, buffer.at[pl.ds(0, SPAN)]), (1, 0, SPAN, buffer.at[pl.ds(SPAN, SPAN)])]


def send_kernel(dest_ref, length_ref, keys_ref, values_ref, queries_ref, a1_ref, a2_ref, b1_ref, b2_ref, ask_ref,
                keys, values, note, load_sem, sem, note_sem):
    first, x = first_survivor(), replica_index()
    loads = []
    for slot in range(SLOTS):
        loads.append((
            pltpu.make_async_copy(keys_ref.at[slot], keys.at[slot], load_sem.at[0, slot]),
            pltpu.make_async_copy(values_ref.at[slot], values.at[slot], load_sem.at[1, slot]),
        ))
    leaves = []
    for slot in range(SLOTS):
        host, _ = places(dest_ref, slot, first)
        leaves.append((host >= 0) & (host != x))
    start_guarded(list(zip(leaves, loads)))
    line = lax.broadcasted_iota(jnp.int32, (NOTE, WIDE), 0)
    guarded = []
    told = [jnp.zeros((NOTE, WIDE), jnp.int32) for _ in range(2)]
    for slot in range(SLOTS):
        host, row = places(dest_ref, slot, first)
        edge = jnp.where(host >= 0, lax.bitwise_xor(host, x), -1)
        along_a = (edge == 1) | (edge == 2)
        along_b = edge == 3
        length = length_ref[slot]
        for n, along in enumerate((along_a, along_b)):
            base = jnp.where(along, row * 3, NOTE)
            for k, value in enumerate((dest_ref[slot] - first + 1, lax.shift_right_logical(length, 4), lax.bitwise_and(length, 15))):
                told[n] = jnp.where(line == base + k, value, told[n])
        for which in range(ROWS):
            mine = row == which
            for guard, parts in (
                (mine & along_a, along_a_pieces(which, a1_ref, a2_ref)),
                (mine & along_b, along_b_pieces(which, b1_ref, b2_ref)),
            ):
                guarded.append((guard, slot, [
                    pltpu.make_async_copy((keys, values)[n].at[slot].at[pl.ds(at, size)], place, sem.at[slot, i])
                    for i, (n, at, size, place) in enumerate(parts)
                ]))
    for n in range(2):
        note[n] = told[n].astype(jnp.float32).astype(jnp.bfloat16)
    notes = [
        pltpu.make_async_copy(note.at[0], a2_ref.at[pl.ds(2 * SPAN - CUT, NOTE)], note_sem.at[0]),
        pltpu.make_async_copy(note.at[1], b2_ref.at[pl.ds(2 * SPAN, NOTE)], note_sem.at[1]),
    ]
    notes.append(pltpu.make_async_copy(queries_ref, ask_ref, note_sem.at[2]))
    for copy in notes:
        copy.start()
    for slot in range(SLOTS):
        wait_guarded([(leaves[slot], loads[slot])])
        start_guarded([(guard, copies) for guard, owner, copies in guarded if owner == slot])
    wait_guarded([(guard, copies) for guard, _, copies in guarded])
    for copy in notes:
        copy.wait()


def send_buffers(destination, lengths, keys, values, queries):
    buffer = lambda rows: jax.ShapeDtypeStruct((rows, WIDE), jnp.bfloat16)
    return pl.pallas_call(
        send_kernel,
        out_shape=[
            buffer(2 * SPAN + CUT), buffer(2 * SPAN - CUT + NOTE), buffer(2 * SPAN), buffer(2 * SPAN + NOTE),
            jax.ShapeDtypeStruct(queries.shape, queries.dtype),
        ],
        in_specs=[SMEM, SMEM, HBM, HBM, VMEM],
        out_specs=[HBM] * 5,
        scratch_shapes=[
            pltpu.VMEM((SLOTS, SPAN, WIDE), jnp.bfloat16),
            pltpu.VMEM((SLOTS, SPAN, WIDE), jnp.bfloat16),
            pltpu.VMEM((2, NOTE, WIDE), jnp.bfloat16),
            pltpu.SemaphoreType.DMA((2, SLOTS)),
            pltpu.SemaphoreType.DMA((SLOTS, 3)),
            pltpu.SemaphoreType.DMA((3,)),
        ],
        compiler_params=pltpu.CompilerParams(vmem_limit_bytes=FULL),
        cost_estimate=pl.CostEstimate(flops=0, bytes_accessed=4 * 2**20, transcendentals=0),
    )(destination, lengths, keys, values, queries)


def start_guarded(guarded):
    for guard, copies in guarded:
        @pl.when(guard)
        def _(copies=copies):
            for copy in copies:
                copy.start()


def wait_guarded(guarded):
    for guard, copies in guarded:
        @pl.when(guard)
        def _(copies=copies):
            for copy in copies:
                copy.wait()


def split_three(x):
    high = x.astype(jnp.bfloat16)
    rest = x - high.astype(jnp.float32)
    middle = rest.astype(jnp.bfloat16)
    low = (rest - middle.astype(jnp.float32)).astype(jnp.bfloat16)
    return high.astype(jnp.float32), middle.astype(jnp.float32), low.astype(jnp.float32)


def heads_of(ref, row):
    block = ref[...].astype(jnp.float32)
    return jnp.concatenate([block[row:row + 1, h * HD:(h + 1) * HD] for h in range(QH)], axis=0)


def spread_heads(query):
    head = lax.broadcasted_iota(jnp.int32, (QH, WIDE), 0)
    lane = lax.broadcasted_iota(jnp.int32, (QH, WIDE), 1)
    wide = jnp.concatenate([query] * KVH, axis=1)
    return jnp.where((head // PER) == (lane // HD), wide, 0.0).astype(jnp.bfloat16)


def block_attention(spread, keys, values, length):
    position = lax.axis_index("t") * SPAN + lax.broadcasted_iota(jnp.int32, (QH, SPAN), 1)
    scores = lax.dot_general(
        spread, keys, (((1,), (1,)), ((), ())), preferred_element_type=jnp.float32
    ) * SCALE
    valid = position < length
    peak = jnp.max(jnp.where(valid, scores, FLOOR), axis=1, keepdims=True)
    weights = jnp.where(valid, jnp.exp(scores - peak), 0.0).astype(jnp.bfloat16)
    mass = jnp.sum(weights.astype(jnp.float32), axis=1, keepdims=True)
    full = jnp.dot(weights, values, preferred_element_type=jnp.float32)
    partial = jnp.concatenate([full[g * PER:(g + 1) * PER, g * HD:(g + 1) * HD] for g in range(KVH)], axis=0)
    return peak, mass, partial.astype(jnp.bfloat16)


def flip(columns):
    lane = lax.broadcasted_iota(jnp.int32, (QH, HD), 1)
    block = jnp.zeros((QH, HD), jnp.float32)
    for n, column in columns.items():
        block = jnp.where(lane == n, column, block)
    return jnp.transpose(jnp.concatenate([block, jnp.zeros((HD - QH, HD), jnp.float32)], axis=0))


def statistics(row, peak, mass):
    columns = {row * STATS + k: piece for k, piece in enumerate(split_three(peak) + split_three(mass))}
    return flip(columns)[:16].astype(jnp.bfloat16)


def mine(row):
    line = lax.broadcasted_iota(jnp.int32, (16, HD), 0)
    return (line >= row * STATS) & (line < (row + 1) * STATS)


def early_kernel(dest_ref, length_ref, asked_ref, queries_ref, new_keys_ref, new_values_ref, keys_ref, values_ref,
                 far_ref, own_ref, own_values_ref, keys, values, sem):
    first, x = first_survivor(), replica_index()
    line = lax.broadcasted_iota(jnp.int32, (NOTE, HD), 0)
    told = jnp.zeros((NOTE, HD), jnp.int32)
    far = []
    guarded = []
    for row in range(ROWS):
        found, length = jnp.int32(-1), jnp.int32(0)
        wanted = lax.bitwise_xor(x, 2) * ROWS + row + first
        for slot in range(SLOTS):
            hit = dest_ref[slot] == wanted
            found = jnp.where(hit, slot, found)
            length = jnp.where(hit, length_ref[slot], length)
        told = jnp.where((line == row * 3) & (found >= 0), wanted - first + 1, told)
        slot = jnp.maximum(found, 0)
        guarded.append((found >= 0, [
            pltpu.make_async_copy(keys_ref.at[slot], keys.at[row], sem.at[row, 0]),
            pltpu.make_async_copy(values_ref.at[slot], values.at[row], sem.at[row, 1]),
        ]))
        far.append((found, length))
    start_guarded(guarded)
    far_ref[PARTIAL:, :] = told.astype(jnp.float32).astype(jnp.bfloat16)
    far_ref[STAT:PARTIAL, :] = jnp.zeros((16, HD), jnp.bfloat16)
    own = {}
    for row in range(ROWS):
        def per_head(ref):
            block = ref[...].astype(jnp.float32)
            return jnp.concatenate([
                jnp.broadcast_to(block[row:row + 1, g * HD:(g + 1) * HD], (PER, HD)) for g in range(KVH)
            ], axis=0)

        own[row] = jnp.sum(heads_of(queries_ref, row) * per_head(new_keys_ref), axis=1, keepdims=True) * SCALE
        own_values_ref[row] = per_head(new_values_ref)
    own_ref[...] = flip(own)[:8]
    wait_guarded(guarded)
    for row, (found, length) in enumerate(far):
        @pl.when(found >= 0)
        def _(row=row, length=length):
            peak, mass, partial = block_attention(spread_heads(heads_of(asked_ref, row)), keys[row], values[row], length)
            far_ref[row * QH:(row + 1) * QH, :] = partial
            far_ref[STAT:PARTIAL, :] = jnp.where(mine(row), statistics(row, peak, mass), far_ref[STAT:PARTIAL, :])


def early(destination, lengths, asked, queries, new_keys, new_values, keys, values):
    return pl.pallas_call(
        early_kernel,
        out_shape=[
            jax.ShapeDtypeStruct((PARTIAL + NOTE, HD), jnp.bfloat16),
            jax.ShapeDtypeStruct((8, HD), jnp.float32),
            jax.ShapeDtypeStruct((ROWS, QH, HD), jnp.float32),
        ],
        in_specs=[SMEM, SMEM] + [VMEM] * 4 + [HBM] * 2,
        out_specs=[VMEM] * 3,
        scratch_shapes=[
            pltpu.VMEM((ROWS, SPAN, WIDE), jnp.bfloat16),
            pltpu.VMEM((ROWS, SPAN, WIDE), jnp.bfloat16),
            pltpu.SemaphoreType.DMA((ROWS, 2)),
        ],
        compiler_params=pltpu.CompilerParams(vmem_limit_bytes=PART),
        cost_estimate=pl.CostEstimate(flops=2**32, bytes_accessed=2**20, transcendentals=2**14),
    )(destination, lengths, asked, queries, new_keys, new_values, keys, values)


def attend_kernel(dest_ref, length_ref, queries_ref, keys_ref, values_ref, a1_ref, a2_ref, b1_ref, b2_ref, far_ref,
                  out_ref, moved_keys_ref, moved_values_ref, stage, pack, spread, sem, moved_sem):
    first, x = first_survivor(), replica_index()
    note_a = a2_ref[2 * SPAN - CUT:, :HD].astype(jnp.float32)
    note_b = b2_ref[2 * SPAN:, :HD].astype(jnp.float32)
    line = lax.broadcasted_iota(jnp.int32, (NOTE, HD), 0)
    rows = []
    guarded = []
    for row in range(ROWS):
        wanted = x * ROWS + row
        here, slot, length = jnp.bool_(False), jnp.int32(0), jnp.int32(0)
        for k in range(SLOTS):
            hit = dest_ref[k] == wanted + first
            here = here | hit
            slot = jnp.where(hit, k, slot)
            length = jnp.where(hit, length_ref[k], length)

        def read(note, k):
            return jnp.max(jnp.where(line == row * 3 + k, note, 0.0)).astype(jnp.int32)

        in_a, in_b = read(note_a, 0) == wanted + 1, read(note_b, 0) == wanted + 1
        length = jnp.where(in_a, read(note_a, 1) * 16 + read(note_a, 2), length)
        length = jnp.where(in_b, read(note_b, 1) * 16 + read(note_b, 2), length)
        rows.append((here | in_a | in_b, length))
        base = 2 * SPAN * row
        for guard, parts in (
            (here, [(0, 0, SPAN, keys_ref.at[slot]), (1, 0, SPAN, values_ref.at[slot])]),
            (in_a, along_a_pieces(row, a1_ref, a2_ref)),
            (in_b, along_b_pieces(row, b1_ref, b2_ref)),
        ):
            guarded.append((guard, [
                pltpu.make_async_copy(place, stage.at[pl.ds(base + n * SPAN + at, size)], sem.at[row, i])
                for i, (n, at, size, place) in enumerate(parts)
            ]))
    start_guarded(guarded)
    pack[...] = far_ref[:PARTIAL, :]
    for row in range(ROWS):
        spread[row] = spread_heads(heads_of(queries_ref, row))
    wait_guarded(guarded)
    moves = []
    for row, (near, _) in enumerate(rows):
        base = 2 * SPAN * row
        moves.append((near, [
            pltpu.make_async_copy(stage.at[pl.ds(base, SPAN)], moved_keys_ref.at[row], moved_sem.at[row, 0]),
            pltpu.make_async_copy(stage.at[pl.ds(base + SPAN, SPAN)], moved_values_ref.at[row], moved_sem.at[row, 1]),
        ]))
    start_guarded(moves)
    results = [
        block_attention(
            spread[row], stage[2 * SPAN * row:2 * SPAN * row + SPAN],
            stage[2 * SPAN * row + SPAN:2 * SPAN * (row + 1)], length,
        )
        for row, (_, length) in enumerate(rows)
    ]
    for row, ((near, _), (peak, mass, partial)) in enumerate(zip(rows, results)):
        @pl.when(near)
        def _(row=row, peak=peak, mass=mass, partial=partial):
            pack[row * QH:(row + 1) * QH, :] = partial
            pack[STAT:PARTIAL, :] = jnp.where(mine(row), statistics(row, peak, mass), pack[STAT:PARTIAL, :])
    for peer in range(TENSOR):
        out_ref[peer] = pack[...]
    wait_guarded(moves)


def attend(destination, lengths, queries, keys, values, a1, a2, b1, b2, far):
    moved = jax.ShapeDtypeStruct((ROWS, SPAN, WIDE), jnp.bfloat16)
    return pl.pallas_call(
        attend_kernel,
        out_shape=[jax.ShapeDtypeStruct((TENSOR, PARTIAL, HD), jnp.bfloat16), moved, moved],
        in_specs=[SMEM, SMEM, VMEM, HBM, HBM, HBM, VMEM, HBM, VMEM, VMEM],
        out_specs=[VMEM, HBM, HBM],
        scratch_shapes=[
            pltpu.VMEM((4 * SPAN, WIDE), jnp.bfloat16),
            pltpu.VMEM((PARTIAL, HD), jnp.bfloat16),
            pltpu.VMEM((ROWS, QH, WIDE), jnp.bfloat16),
            pltpu.SemaphoreType.DMA((ROWS, 3)),
            pltpu.SemaphoreType.DMA((ROWS, 2)),
        ],
        compiler_params=pltpu.CompilerParams(vmem_limit_bytes=PART),
        cost_estimate=pl.CostEstimate(flops=2**31, bytes_accessed=2 * 2**20, transcendentals=2**14),
    )(destination, lengths, queries, keys, values, a1, a2, b1, b2, far)


def relayed_kernel(far_ref, c1_ref, c2_ref, keys_in_ref, values_in_ref, moved_keys_ref, moved_values_ref, sem):
    x = replica_index()
    note = far_ref[PARTIAL:, :].astype(jnp.float32)
    line = lax.broadcasted_iota(jnp.int32, (NOTE, HD), 0)
    guarded = []
    for row in range(ROWS):
        told = jnp.max(jnp.where(line == row * 3, note, 0.0)).astype(jnp.int32)
        guarded.append((told == x * ROWS + row + 1, [
            pltpu.make_async_copy(place, (moved_keys_ref, moved_values_ref)[n].at[row].at[pl.ds(at, size)], sem.at[row, i])
            for i, (n, at, size, place) in enumerate(along_a_pieces(row, c1_ref, c2_ref))
        ]))
    start_guarded(guarded)
    wait_guarded(guarded)


def place_relayed(far, c1, c2, moved_keys, moved_values):
    moved = jax.ShapeDtypeStruct((ROWS, SPAN, WIDE), jnp.bfloat16)
    return pl.pallas_call(
        relayed_kernel,
        out_shape=[moved, moved],
        in_specs=[VMEM] * 3 + [HBM] * 2,
        out_specs=[HBM, HBM],
        input_output_aliases={3: 0, 4: 1},
        scratch_shapes=[pltpu.SemaphoreType.DMA((ROWS, 3))],
        compiler_params=pltpu.CompilerParams(vmem_limit_bytes=PART),
        cost_estimate=pl.CostEstimate(flops=0, bytes_accessed=2**20, transcendentals=0),
    )(far, c1, c2, moved_keys, moved_values)


def finish_kernel(blocks_ref, own_ref, own_values_ref, attended_ref):
    stats = [blocks_ref[b, STAT:PARTIAL, :].astype(jnp.float32) for b in range(TENSOR)]
    columns = []
    for row in range(ROWS):
        at = row * STATS
        peaks = [(one[at:at + 1] + one[at + 1:at + 2]) + one[at + 2:at + 3] for one in stats]
        masses = [(one[at + 3:at + 4] + one[at + 4:at + 5]) + one[at + 5:at + 6] for one in stats]
        own = own_ref[row:row + 1, :]
        top = functools.reduce(jnp.maximum, peaks, own)
        fades = [jnp.exp(peak - top) for peak in peaks]
        own_weight = jnp.exp(own - top)
        denominator = own_weight
        for fade, mass in zip(fades, masses):
            denominator = denominator + fade * mass
        columns += [one / denominator for one in fades + [own_weight]]
    columns.append(jnp.zeros((HD - len(columns), HD), jnp.float32))
    shares = jnp.transpose(jnp.concatenate(columns, axis=0))[:QH]
    parts = []
    for row in range(ROWS):
        at = row * (TENSOR + 1)
        total = shares[:, at + TENSOR:at + TENSOR + 1] * own_values_ref[row]
        for b in range(TENSOR):
            total = total + shares[:, at + b:at + b + 1] * blocks_ref[b, row * QH:(row + 1) * QH, :].astype(jnp.float32)
        parts.append(total)
    for head in range(QH):
        both = jnp.concatenate([part[head:head + 1] for part in parts], axis=0)
        attended_ref[:, head * HD:(head + 1) * HD] = both.astype(jnp.bfloat16)


def finish(blocks, own, own_values):
    return pl.pallas_call(
        finish_kernel,
        out_shape=jax.ShapeDtypeStruct((ROWS, QH * HD), jnp.bfloat16),
        in_specs=[VMEM] * 3,
        out_specs=VMEM,
        compiler_params=pltpu.CompilerParams(vmem_limit_bytes=PART),
        cost_estimate=pl.CostEstimate(flops=2**20, bytes_accessed=2**20, transcendentals=2**16),
    )(blocks, own, own_values)


def on_device(keys, values, lengths, destination, queries, new_keys, new_values):
    a1, a2, b1, b2, ask = send_buffers(destination, lengths, keys, values, queries)
    asked = lax.ppermute(ask, "x", ASK_C)
    a1 = lax.ppermute(a1, "x", EDGE_A)
    a2 = lax.ppermute(a2, "x", EDGE_A)
    b1 = lax.ppermute(b1, "x", EDGE_B)
    b2 = lax.ppermute(b2, "x", EDGE_B)
    far, own, own_values = early(destination, lengths, asked, queries, new_keys, new_values, keys, values)
    far = lax.ppermute(far, "x", EDGE_C)
    c1 = lax.ppermute(a1, "x", RELAY)
    c2 = lax.ppermute(a2, "x", RELAY)
    partial, moved_keys, moved_values = attend(destination, lengths, queries, keys, values, a1, a2, b1, b2, far)
    blocks = lax.all_to_all(partial, "t", 0, 0)
    moved_keys, moved_values = place_relayed(far, c1, c2, moved_keys, moved_values)
    attended = finish(blocks, own, own_values)
    return moved_keys, moved_values, attended


def solution(mesh):
    groups = Mesh(mesh.devices.reshape(-1, GROUP, TENSOR), ("z", "x", "t"))
    dp = ("z", "x")
    return jax.shard_map(
        on_device,
        mesh=groups,
        in_specs=(P(dp, "t", None), P(dp, "t", None), P(dp), P(dp), P(dp, None), P(dp, None), P(dp, None)),
        out_specs=(P(dp, "t", None), P(dp, "t", None), P(dp, None)),
        check_vma=False,
    )
```

```python
import functools

import jax
import jax.numpy as jnp
from jax import lax
from jax.experimental import pallas as pl
from jax.experimental.pallas import tpu as pltpu
from jax.sharding import Mesh
from jax.sharding import PartitionSpec as P

QH = 64
KVH = 8
HD = 128
SLOTS = 4
ROWS = 2
GROUP = 4
PER = QH // KVH
TENSOR = 8
SPAN = 128
WIDE = KVH * HD
SCALE = HD ** -0.5
FLOOR = -1e30

STAT = ROWS * QH
STATS = 6
PARTIAL = STAT + 16
NOTE = 16
EDGE_A = ((0, 1), (1, 0), (2, 3), (3, 2))
EDGE_B = ((1, 2), (2, 1))
EDGE_C = ((1, 3), (2, 0))
RELAY = ((0, 3), (3, 0))
ASK_C = ((3, 1), (0, 2))

CUT = 64

FULL = 60 * 2**20
PART = 16 * 2**20

SMEM = pl.BlockSpec(memory_space=pltpu.SMEM)
VMEM = pl.BlockSpec(memory_space=pltpu.VMEM)
HBM = pl.BlockSpec(memory_space=pltpu.HBM)


def replica_index():
    return lax.axis_index("x")


def first_survivor():
    return lax.axis_index("z") * (GROUP * ROWS)


def places(dest_ref, slot, first):
    local = dest_ref[slot] - first
    live = dest_ref[slot] >= 0
    return jnp.where(live, lax.shift_right_arithmetic(local, 1), -1), lax.bitwise_and(local, 1)


def along_a_pieces(row, a1_ref, a2_ref):
    if row == 0:
        return [(0, 0, SPAN, a1_ref.at[pl.ds(0, SPAN)]), (1, 0, SPAN, a1_ref.at[pl.ds(SPAN, SPAN)])]
    return [
        (0, 0, CUT, a1_ref.at[pl.ds(2 * SPAN, CUT)]),
        (0, CUT, SPAN - CUT, a2_ref.at[pl.ds(0, SPAN - CUT)]),
        (1, 0, SPAN, a2_ref.at[pl.ds(SPAN - CUT, SPAN)]),
    ]


def along_b_pieces(row, b1_ref, b2_ref):
    buffer = (b1_ref, b2_ref)[row]
    return [(0, 0, SPAN, buffer.at[pl.ds(0, SPAN)]), (1, 0, SPAN, buffer.at[pl.ds(SPAN, SPAN)])]


def send_kernel(dest_ref, length_ref, keys_ref, values_ref, queries_ref, a1_ref, a2_ref, b1_ref, b2_ref, ask_ref,
                keys, values, note, load_sem, sem, note_sem):
    first, x = first_survivor(), replica_index()
    loads = []
    for slot in range(SLOTS):
        loads.append((
            pltpu.make_async_copy(keys_ref.at[slot], keys.at[slot], load_sem.at[0, slot]),
            pltpu.make_async_copy(values_ref.at[slot], values.at[slot], load_sem.at[1, slot]),
        ))
    leaves = []
    for slot in range(SLOTS):
        host, _ = places(dest_ref, slot, first)
        leaves.append((host >= 0) & (host != x))
    start_guarded(list(zip(leaves, loads)))
    line = lax.broadcasted_iota(jnp.int32, (NOTE, WIDE), 0)
    guarded = []
    told = [jnp.zeros((NOTE, WIDE), jnp.int32) for _ in range(2)]
    for slot in range(SLOTS):
        host, row = places(dest_ref, slot, first)
        edge = jnp.where(host >= 0, lax.bitwise_xor(host, x), -1)
        along_a = (edge == 1) | (edge == 2)
        along_b = edge == 3
        length = length_ref[slot]
        for n, along in enumerate((along_a, along_b)):
            base = jnp.where(along, row * 3, NOTE)
            for k, value in enumerate((dest_ref[slot] - first + 1, lax.shift_right_logical(length, 4), lax.bitwise_and(length, 15))):
                told[n] = jnp.where(line == base + k, value, told[n])
        for which in range(ROWS):
            mine = row == which
            for guard, parts in (
                (mine & along_a, along_a_pieces(which, a1_ref, a2_ref)),
                (mine & along_b, along_b_pieces(which, b1_ref, b2_ref)),
            ):
                for i, (n, at, size, place) in enumerate(parts):
                    guarded.append((guard, (slot, n), [
                        pltpu.make_async_copy((keys, values)[n].at[slot].at[pl.ds(at, size)], place, sem.at[slot, i])
                    ]))
    for n in range(2):
        note[n] = told[n].astype(jnp.float32).astype(jnp.bfloat16)
    notes = [
        pltpu.make_async_copy(note.at[0], a2_ref.at[pl.ds(2 * SPAN - CUT, NOTE)], note_sem.at[0]),
        pltpu.make_async_copy(note.at[1], b2_ref.at[pl.ds(2 * SPAN, NOTE)], note_sem.at[1]),
    ]
    notes.append(pltpu.make_async_copy(queries_ref, ask_ref, note_sem.at[2]))
    for copy in notes:
        copy.start()
    for slot in range(SLOTS):
        for n in range(2):
            wait_guarded([(leaves[slot], [loads[slot][n]])])
            start_guarded([(guard, copies) for guard, owner, copies in guarded if owner == (slot, n)])
    wait_guarded([(guard, copies) for guard, _, copies in guarded])
    for copy in notes:
        copy.wait()


def send_buffers(destination, lengths, keys, values, queries):
    buffer = lambda rows: jax.ShapeDtypeStruct((rows, WIDE), jnp.bfloat16)
    return pl.pallas_call(
        send_kernel,
        out_shape=[
            buffer(2 * SPAN + CUT), buffer(2 * SPAN - CUT + NOTE), buffer(2 * SPAN), buffer(2 * SPAN + NOTE),
            jax.ShapeDtypeStruct(queries.shape, queries.dtype),
        ],
        in_specs=[SMEM, SMEM, HBM, HBM, VMEM],
        out_specs=[HBM] * 5,
        scratch_shapes=[
            pltpu.VMEM((SLOTS, SPAN, WIDE), jnp.bfloat16),
            pltpu.VMEM((SLOTS, SPAN, WIDE), jnp.bfloat16),
            pltpu.VMEM((2, NOTE, WIDE), jnp.bfloat16),
            pltpu.SemaphoreType.DMA((2, SLOTS)),
            pltpu.SemaphoreType.DMA((SLOTS, 3)),
            pltpu.SemaphoreType.DMA((3,)),
        ],
        compiler_params=pltpu.CompilerParams(vmem_limit_bytes=FULL),
        cost_estimate=pl.CostEstimate(flops=0, bytes_accessed=4 * 2**20, transcendentals=0),
    )(destination, lengths, keys, values, queries)


def start_guarded(guarded):
    for guard, copies in guarded:
        @pl.when(guard)
        def _(copies=copies):
            for copy in copies:
                copy.start()


def wait_guarded(guarded):
    for guard, copies in guarded:
        @pl.when(guard)
        def _(copies=copies):
            for copy in copies:
                copy.wait()


def split_three(x):
    high = x.astype(jnp.bfloat16)
    rest = x - high.astype(jnp.float32)
    middle = rest.astype(jnp.bfloat16)
    low = (rest - middle.astype(jnp.float32)).astype(jnp.bfloat16)
    return high.astype(jnp.float32), middle.astype(jnp.float32), low.astype(jnp.float32)


def heads_of(ref, row):
    block = ref[...].astype(jnp.float32)
    return jnp.concatenate([block[row:row + 1, h * HD:(h + 1) * HD] for h in range(QH)], axis=0)


def spread_heads(query):
    head = lax.broadcasted_iota(jnp.int32, (QH, WIDE), 0)
    lane = lax.broadcasted_iota(jnp.int32, (QH, WIDE), 1)
    wide = jnp.concatenate([query] * KVH, axis=1)
    return jnp.where((head // PER) == (lane // HD), wide, 0.0).astype(jnp.bfloat16)


def block_attention(spread, keys, values, length):
    position = lax.axis_index("t") * SPAN + lax.broadcasted_iota(jnp.int32, (QH, SPAN), 1)
    scores = lax.dot_general(
        spread, keys, (((1,), (1,)), ((), ())), preferred_element_type=jnp.float32
    ) * SCALE
    valid = position < length
    peak = jnp.max(jnp.where(valid, scores, FLOOR), axis=1, keepdims=True)
    weights = jnp.where(valid, jnp.exp(scores - peak), 0.0).astype(jnp.bfloat16)
    mass = jnp.sum(weights.astype(jnp.float32), axis=1, keepdims=True)
    full = jnp.dot(weights, values, preferred_element_type=jnp.float32)
    partial = jnp.concatenate([full[g * PER:(g + 1) * PER, g * HD:(g + 1) * HD] for g in range(KVH)], axis=0)
    return peak, mass, partial.astype(jnp.bfloat16)


def flip(columns):
    lane = lax.broadcasted_iota(jnp.int32, (QH, HD), 1)
    block = jnp.zeros((QH, HD), jnp.float32)
    for n, column in columns.items():
        block = jnp.where(lane == n, column, block)
    return jnp.transpose(jnp.concatenate([block, jnp.zeros((HD - QH, HD), jnp.float32)], axis=0))


def statistics(row, peak, mass):
    columns = {row * STATS + k: piece for k, piece in enumerate(split_three(peak) + split_three(mass))}
    return flip(columns)[:16].astype(jnp.bfloat16)


def mine(row):
    line = lax.broadcasted_iota(jnp.int32, (16, HD), 0)
    return (line >= row * STATS) & (line < (row + 1) * STATS)


def early_kernel(dest_ref, length_ref, asked_ref, queries_ref, new_keys_ref, new_values_ref, keys_ref, values_ref,
                 far_ref, own_ref, own_values_ref, keys, values, sem):
    first, x = first_survivor(), replica_index()
    line = lax.broadcasted_iota(jnp.int32, (NOTE, HD), 0)
    told = jnp.zeros((NOTE, HD), jnp.int32)
    far = []
    guarded = []
    for row in range(ROWS):
        found, length = jnp.int32(-1), jnp.int32(0)
        wanted = lax.bitwise_xor(x, 2) * ROWS + row + first
        for slot in range(SLOTS):
            hit = dest_ref[slot] == wanted
            found = jnp.where(hit, slot, found)
            length = jnp.where(hit, length_ref[slot], length)
        told = jnp.where((line == row * 3) & (found >= 0), wanted - first + 1, told)
        slot = jnp.maximum(found, 0)
        guarded.append((found >= 0, [
            pltpu.make_async_copy(keys_ref.at[slot], keys.at[row], sem.at[row, 0]),
            pltpu.make_async_copy(values_ref.at[slot], values.at[row], sem.at[row, 1]),
        ]))
        far.append((found, length))
    start_guarded(guarded)
    far_ref[PARTIAL:, :] = told.astype(jnp.float32).astype(jnp.bfloat16)
    far_ref[STAT:PARTIAL, :] = jnp.zeros((16, HD), jnp.bfloat16)
    own = {}
    for row in range(ROWS):
        def per_head(ref):
            block = ref[...].astype(jnp.float32)
            return jnp.concatenate([
                jnp.broadcast_to(block[row:row + 1, g * HD:(g + 1) * HD], (PER, HD)) for g in range(KVH)
            ], axis=0)

        own[row] = jnp.sum(heads_of(queries_ref, row) * per_head(new_keys_ref), axis=1, keepdims=True) * SCALE
        own_values_ref[row] = per_head(new_values_ref)
    own_ref[...] = flip(own)[:8]
    wait_guarded(guarded)
    for row, (found, length) in enumerate(far):
        @pl.when(found >= 0)
        def _(row=row, length=length):
            peak, mass, partial = block_attention(spread_heads(heads_of(asked_ref, row)), keys[row], values[row], length)
            far_ref[row * QH:(row + 1) * QH, :] = partial
            far_ref[STAT:PARTIAL, :] = jnp.where(mine(row), statistics(row, peak, mass), far_ref[STAT:PARTIAL, :])


def early(destination, lengths, asked, queries, new_keys, new_values, keys, values):
    return pl.pallas_call(
        early_kernel,
        out_shape=[
            jax.ShapeDtypeStruct((PARTIAL + NOTE, HD), jnp.bfloat16),
            jax.ShapeDtypeStruct((8, HD), jnp.float32),
            jax.ShapeDtypeStruct((ROWS, QH, HD), jnp.float32),
        ],
        in_specs=[SMEM, SMEM] + [VMEM] * 4 + [HBM] * 2,
        out_specs=[VMEM] * 3,
        scratch_shapes=[
            pltpu.VMEM((ROWS, SPAN, WIDE), jnp.bfloat16),
            pltpu.VMEM((ROWS, SPAN, WIDE), jnp.bfloat16),
            pltpu.SemaphoreType.DMA((ROWS, 2)),
        ],
        compiler_params=pltpu.CompilerParams(vmem_limit_bytes=PART),
        cost_estimate=pl.CostEstimate(flops=2**32, bytes_accessed=2**20, transcendentals=2**14),
    )(destination, lengths, asked, queries, new_keys, new_values, keys, values)


def attend_kernel(dest_ref, length_ref, queries_ref, keys_ref, values_ref, a1_ref, a2_ref, b1_ref, b2_ref, far_ref,
                  out_ref, moved_keys_ref, moved_values_ref, stage, pack, spread, sem, moved_sem):
    first, x = first_survivor(), replica_index()
    note_a = a2_ref[2 * SPAN - CUT:, :HD].astype(jnp.float32)
    note_b = b2_ref[2 * SPAN:, :HD].astype(jnp.float32)
    line = lax.broadcasted_iota(jnp.int32, (NOTE, HD), 0)
    rows = []
    guarded = []
    for row in range(ROWS):
        wanted = x * ROWS + row
        here, slot, length = jnp.bool_(False), jnp.int32(0), jnp.int32(0)
        for k in range(SLOTS):
            hit = dest_ref[k] == wanted + first
            here = here | hit
            slot = jnp.where(hit, k, slot)
            length = jnp.where(hit, length_ref[k], length)

        def read(note, k):
            return jnp.max(jnp.where(line == row * 3 + k, note, 0.0)).astype(jnp.int32)

        in_a, in_b = read(note_a, 0) == wanted + 1, read(note_b, 0) == wanted + 1
        length = jnp.where(in_a, read(note_a, 1) * 16 + read(note_a, 2), length)
        length = jnp.where(in_b, read(note_b, 1) * 16 + read(note_b, 2), length)
        rows.append((here | in_a | in_b, length))
        base = 2 * SPAN * row
        for guard, parts in (
            (here, [(0, 0, SPAN, keys_ref.at[slot]), (1, 0, SPAN, values_ref.at[slot])]),
            (in_a, along_a_pieces(row, a1_ref, a2_ref)),
            (in_b, along_b_pieces(row, b1_ref, b2_ref)),
        ):
            guarded.append((guard, [
                pltpu.make_async_copy(place, stage.at[pl.ds(base + n * SPAN + at, size)], sem.at[row, i])
                for i, (n, at, size, place) in enumerate(parts)
            ]))
    start_guarded(guarded)
    pack[...] = far_ref[:PARTIAL, :]
    for row in range(ROWS):
        spread[row] = spread_heads(heads_of(queries_ref, row))
    wait_guarded(guarded)
    moves = []
    for row, (near, _) in enumerate(rows):
        base = 2 * SPAN * row
        moves.append((near, [
            pltpu.make_async_copy(stage.at[pl.ds(base, SPAN)], moved_keys_ref.at[row], moved_sem.at[row, 0]),
            pltpu.make_async_copy(stage.at[pl.ds(base + SPAN, SPAN)], moved_values_ref.at[row], moved_sem.at[row, 1]),
        ]))
    start_guarded(moves)
    results = [
        block_attention(
            spread[row], stage[2 * SPAN * row:2 * SPAN * row + SPAN],
            stage[2 * SPAN * row + SPAN:2 * SPAN * (row + 1)], length,
        )
        for row, (_, length) in enumerate(rows)
    ]
    for row, ((near, _), (peak, mass, partial)) in enumerate(zip(rows, results)):
        @pl.when(near)
        def _(row=row, peak=peak, mass=mass, partial=partial):
            pack[row * QH:(row + 1) * QH, :] = partial
            pack[STAT:PARTIAL, :] = jnp.where(mine(row), statistics(row, peak, mass), pack[STAT:PARTIAL, :])
    for peer in range(TENSOR):
        out_ref[peer] = pack[...]
    wait_guarded(moves)


def attend(destination, lengths, queries, keys, values, a1, a2, b1, b2, far):
    moved = jax.ShapeDtypeStruct((ROWS, SPAN, WIDE), jnp.bfloat16)
    return pl.pallas_call(
        attend_kernel,
        out_shape=[jax.ShapeDtypeStruct((TENSOR, PARTIAL, HD), jnp.bfloat16), moved, moved],
        in_specs=[SMEM, SMEM, VMEM, HBM, HBM, HBM, VMEM, HBM, VMEM, VMEM],
        out_specs=[VMEM, HBM, HBM],
        scratch_shapes=[
            pltpu.VMEM((4 * SPAN, WIDE), jnp.bfloat16),
            pltpu.VMEM((PARTIAL, HD), jnp.bfloat16),
            pltpu.VMEM((ROWS, QH, WIDE), jnp.bfloat16),
            pltpu.SemaphoreType.DMA((ROWS, 3)),
            pltpu.SemaphoreType.DMA((ROWS, 2)),
        ],
        compiler_params=pltpu.CompilerParams(vmem_limit_bytes=PART),
        cost_estimate=pl.CostEstimate(flops=2**31, bytes_accessed=2 * 2**20, transcendentals=2**14),
    )(destination, lengths, queries, keys, values, a1, a2, b1, b2, far)


def relayed_kernel(far_ref, c1_ref, c2_ref, keys_in_ref, values_in_ref, moved_keys_ref, moved_values_ref, sem):
    x = replica_index()
    note = far_ref[PARTIAL:, :].astype(jnp.float32)
    line = lax.broadcasted_iota(jnp.int32, (NOTE, HD), 0)
    guarded = []
    for row in range(ROWS):
        told = jnp.max(jnp.where(line == row * 3, note, 0.0)).astype(jnp.int32)
        guarded.append((told == x * ROWS + row + 1, [
            pltpu.make_async_copy(place, (moved_keys_ref, moved_values_ref)[n].at[row].at[pl.ds(at, size)], sem.at[row, i])
            for i, (n, at, size, place) in enumerate(along_a_pieces(row, c1_ref, c2_ref))
        ]))
    start_guarded(guarded)
    wait_guarded(guarded)


def place_relayed(far, c1, c2, moved_keys, moved_values):
    moved = jax.ShapeDtypeStruct((ROWS, SPAN, WIDE), jnp.bfloat16)
    return pl.pallas_call(
        relayed_kernel,
        out_shape=[moved, moved],
        in_specs=[VMEM] * 3 + [HBM] * 2,
        out_specs=[HBM, HBM],
        input_output_aliases={3: 0, 4: 1},
        scratch_shapes=[pltpu.SemaphoreType.DMA((ROWS, 3))],
        compiler_params=pltpu.CompilerParams(vmem_limit_bytes=PART),
        cost_estimate=pl.CostEstimate(flops=0, bytes_accessed=2**20, transcendentals=0),
    )(far, c1, c2, moved_keys, moved_values)


def finish_kernel(blocks_ref, own_ref, own_values_ref, attended_ref):
    stats = [blocks_ref[b, STAT:PARTIAL, :].astype(jnp.float32) for b in range(TENSOR)]
    columns = []
    for row in range(ROWS):
        at = row * STATS
        peaks = [(one[at:at + 1] + one[at + 1:at + 2]) + one[at + 2:at + 3] for one in stats]
        masses = [(one[at + 3:at + 4] + one[at + 4:at + 5]) + one[at + 5:at + 6] for one in stats]
        own = own_ref[row:row + 1, :]
        top = functools.reduce(jnp.maximum, peaks, own)
        fades = [jnp.exp(peak - top) for peak in peaks]
        own_weight = jnp.exp(own - top)
        denominator = own_weight
        for fade, mass in zip(fades, masses):
            denominator = denominator + fade * mass
        columns += [one / denominator for one in fades + [own_weight]]
    columns.append(jnp.zeros((HD - len(columns), HD), jnp.float32))
    shares = jnp.transpose(jnp.concatenate(columns, axis=0))[:QH]
    parts = []
    for row in range(ROWS):
        at = row * (TENSOR + 1)
        total = shares[:, at + TENSOR:at + TENSOR + 1] * own_values_ref[row]
        for b in range(TENSOR):
            total = total + shares[:, at + b:at + b + 1] * blocks_ref[b, row * QH:(row + 1) * QH, :].astype(jnp.float32)
        parts.append(total)
    for head in range(QH):
        both = jnp.concatenate([part[head:head + 1] for part in parts], axis=0)
        attended_ref[:, head * HD:(head + 1) * HD] = both.astype(jnp.bfloat16)


def finish(blocks, own, own_values):
    return pl.pallas_call(
        finish_kernel,
        out_shape=jax.ShapeDtypeStruct((ROWS, QH * HD), jnp.bfloat16),
        in_specs=[VMEM] * 3,
        out_specs=VMEM,
        compiler_params=pltpu.CompilerParams(vmem_limit_bytes=PART),
        cost_estimate=pl.CostEstimate(flops=2**20, bytes_accessed=2**20, transcendentals=2**16),
    )(blocks, own, own_values)


def on_device(keys, values, lengths, destination, queries, new_keys, new_values):
    a1, a2, b1, b2, ask = send_buffers(destination, lengths, keys, values, queries)
    asked = lax.ppermute(ask, "x", ASK_C)
    a1 = lax.ppermute(a1, "x", EDGE_A)
    a2 = lax.ppermute(a2, "x", EDGE_A)
    b1 = lax.ppermute(b1, "x", EDGE_B)
    b2 = lax.ppermute(b2, "x", EDGE_B)
    far, own, own_values = early(destination, lengths, asked, queries, new_keys, new_values, keys, values)
    far = lax.ppermute(far, "x", EDGE_C)
    c1 = lax.ppermute(a1, "x", RELAY)
    c2 = lax.ppermute(a2, "x", RELAY)
    partial, moved_keys, moved_values = attend(destination, lengths, queries, keys, values, a1, a2, b1, b2, far)
    blocks = lax.all_to_all(partial, "t", 0, 0)
    moved_keys, moved_values = place_relayed(far, c1, c2, moved_keys, moved_values)
    attended = finish(blocks, own, own_values)
    return moved_keys, moved_values, attended


def solution(mesh):
    groups = Mesh(mesh.devices.reshape(-1, GROUP, TENSOR), ("z", "x", "t"))
    dp = ("z", "x")
    return jax.shard_map(
        on_device,
        mesh=groups,
        in_specs=(P(dp, "t", None), P(dp, "t", None), P(dp), P(dp), P(dp, None), P(dp, None), P(dp, None)),
        out_specs=(P(dp, "t", None), P(dp, "t", None), P(dp, None)),
        check_vma=False,
    )
```
